256 devices in a mesh: clus: 32 (over x, y, core), probe: 8 (over z).
Axes of the slice: x: 4, y: 4, z: 8, core: 2. Of those that a mesh axis runs over, the one named last changes fastest.
Arguments:
- probes: bfloat16 [384, 128, 128], P('clus', 'probe'), may hold values from -6 to 6
- onsite: float32 [384, 128], P('clus'), may hold values from -1.1 to 1.1
- hopping: bfloat16 [20, 384, 128, 128], P(None, 'clus'), may hold values from -0.0390625 to 0.0390625
- block_col: int32 [20, 384], P(None, 'clus'), may hold values from -1 to 383, as said below
- atom_of: int32 [384, 128], P('clus'), may hold values from 0 to 31, as said below
- bond_dir: bfloat16 [3, 20, 384], P(None, None, 'clus'), may hold values from -1 to 1, as said below
- chemical_potential: float32 [1], replicated, may hold values from -0.3 to 0.3
Outputs:
- density: float32 [384, 128], P('clus')
- filling: float32 [1], replicated
- forces: float32 [3, 12288], P(None, 'clus')
The draws below stay inside these ranges and needn't reach their ends.
Inputs may be any that keep to these rules, and one draw needn't show every extreme that they name: `block_col`: -1 marks an empty slot. Slot (m, c) belongs to row cluster c; a live slot's column cluster lies within 12 clusters of c, and the live columns of one row cluster are distinct. In each aligned group of 12 row clusters the live slots are those with m under a count common to the group, either 20 or from 5 to 10, except columns that would fall outside the grid, which are empty. In some group, never the first or the last, every slot is live. `atom_of`: in each cluster every atom number appears for exactly four orbitals. `bond_dir`: the three components of each slot form a unit vector.
All inputs are finite; a program needn't handle non-finite values.
Results may differ from the reference program's by a relative error of at most 0.0011.
Values may be sent and summed in bfloat16 or wider, within the bound.
A program may use at most 128 MiB of HBM per device.

```python
import jax
import jax.numpy as jnp
from jax import lax

CL_DEV = 12
BLOCK = 128
ATOMS = 32
NB_FULL = 20
REACH = 12
PROBE_VECTORS = 128
ORDER = 4
NCLUS = 384


def draw_onsite(key, part):
    position = (jnp.arange(NCLUS, dtype=jnp.float32)[:, None] + 0.5) / NCLUS
    profile = 0.45 - 0.9 * position
    rough = jnp.clip(0.25 * jax.random.normal(key, (NCLUS, BLOCK), jnp.float32), -0.6, 0.6)
    return (profile + rough).astype(jnp.float32)


def draw_block_col(key, part):
    groups = NCLUS // CL_DEV
    busy_key, count_key, shuffle_key = jax.random.split(key, 3)
    busy_group = jax.random.randint(busy_key, (), 1, groups - 1)
    counts = jax.random.randint(count_key, (groups,), NB_FULL // 4, NB_FULL // 2 + 1)
    counts = jnp.where(jnp.arange(groups) == busy_group, NB_FULL, counts)
    cluster_count = jnp.repeat(counts, CL_DEV)
    cluster_keys = jax.random.split(shuffle_key, NCLUS)

    def shuffle_one(sub_key):
        return jax.random.permutation(sub_key, 2 * REACH + 1)
    shuffled = jax.vmap(shuffle_one)(cluster_keys)
    offsets = shuffled[:, :NB_FULL] - REACH
    row_index = jnp.arange(NCLUS)[:, None]
    col_index = row_index + offsets
    slot_index = jnp.arange(NB_FULL)[None, :]
    live_slot = (slot_index < cluster_count[:, None]) & (col_index >= 0) & (col_index < NCLUS)
    return jnp.where(live_slot, col_index, -1).T.astype(jnp.int32)


def draw_atom_of(key, part):
    cluster_keys = jax.random.split(key, NCLUS)

    def shuffle_one(sub_key):
        return jax.random.permutation(sub_key, BLOCK) // (BLOCK // ATOMS)
    return jax.vmap(shuffle_one)(cluster_keys).astype(jnp.int32)


def draw_bond_dir(key, part):
    first_key, second_key = jax.random.split(key)
    azimuth = jax.random.uniform(first_key, (NB_FULL, NCLUS), jnp.float32, -jnp.pi, jnp.pi)
    height = jnp.tanh(jax.random.normal(second_key, (NB_FULL, NCLUS), jnp.float32))
    radial = jnp.sqrt(jnp.maximum(1.0 - height * height, 0.0))
    return jnp.stack([radial * jnp.cos(azimuth), radial * jnp.sin(azimuth), height]).astype(jnp.bfloat16)


def level_of(own_key, shape, pieces, low, largest):
    gain = 1.0
    for dim, blocks in pieces:
        draws = jax.random.uniform(jax.random.fold_in(jax.random.fold_in(own_key, 6), dim), (blocks,), jnp.float32, low / len(pieces), largest / len(pieces))
        gain = gain * jnp.repeat(jnp.exp(draws), shape[dim] // blocks).reshape((-1,) + (1,) * (len(shape) - 1 - dim))
    return gain


def noise(key, dims, width, limit, cuts=(), kind=jnp.bfloat16):
    loudness = level_of(key, dims, cuts, -0.22, 0.18) if cuts else 1.0
    values = jax.random.normal(key, dims, jnp.float32) * width * loudness
    return jnp.minimum(jnp.maximum(values, -limit), limit).astype(kind)


def setup_inputs(seed: int = 0) -> dict:
    keys = jax.random.split(jax.random.key(seed), 8)
    probes = noise(keys[0], (NCLUS, PROBE_VECTORS, BLOCK), 1.0, 6.0, ((0, 32), (1, 8)))
    onsite = draw_onsite(jax.random.fold_in(keys[7], 71), 0)
    hopping = noise(keys[2], (NB_FULL, NCLUS, BLOCK, BLOCK), (8 * BLOCK * NB_FULL) ** -0.5, 0.0390625, ((1, 32),))
    block_col = draw_block_col(jax.random.fold_in(keys[7], 71), 0)
    atom_of = draw_atom_of(jax.random.fold_in(keys[7], 71), 0)
    bond_dir = draw_bond_dir(jax.random.fold_in(keys[7], 71), 0)
    chemical_potential = jnp.clip(jax.random.uniform(keys[6], (1,), jnp.float32, -0.3, 0.3), -0.3, 0.3)
    return dict(probes=probes, onsite=onsite, hopping=hopping, block_col=block_col, atom_of=atom_of, bond_dir=bond_dir, chemical_potential=chemical_potential)


DECAY = 50.0
SMEARING_TEMP = 0.1
quad_nodes = 64


def expansion(chemical_potential, degree):
    node_index = jnp.arange(quad_nodes, dtype=jnp.float32)
    bond_angles = jnp.pi * (node_index + 0.5) / quad_nodes
    fermi_occupation = 1.0 / (1.0 + jnp.exp((jnp.cos(bond_angles) - chemical_potential) / SMEARING_TEMP))
    orders = jnp.arange(degree + 1, dtype=jnp.float32)
    cosines = jnp.cos(orders[:, None] * bond_angles[None, :])
    coeffs = (2.0 / quad_nodes) * jnp.sum(cosines * fermi_occupation[None, :], axis=1)
    return coeffs * jnp.where(orders == 0.0, 0.5, 1.0)


def reference(probes, onsite, hopping, block_col, atom_of, bond_dir, chemical_potential):
    live_mask = block_col >= 0
    masked = jnp.where(live_mask[:, :, None, None], hopping, jnp.zeros((), hopping.dtype))
    target_ids = jnp.where(live_mask, block_col, NCLUS).astype(jnp.int32)
    safe_ids = jnp.clip(block_col, 0, NCLUS - 1).astype(jnp.int32)
    highest = lax.Precision.HIGHEST

    def operate(vector_b):
        wide = vector_b.astype(jnp.float32)

        def single_slab(total, slab):
            blocks, gather_ids, targets = slab
            blocks_wide = blocks.astype(jnp.float32)
            picked = jnp.take(wide, gather_ids, axis=0)
            direct = jnp.einsum("cpj,cij->cpi", picked, blocks_wide, precision=highest)
            spread = jnp.einsum("cpi,cij->cpj", wide, blocks_wide, precision=highest)
            carried = jax.ops.segment_sum(spread, targets, num_segments=NCLUS + 1)[:NCLUS]
            return total + direct + carried, None

        total, unused = lax.scan(single_slab, jnp.zeros(wide.shape, jnp.float32), (masked, safe_ids, target_ids))
        return onsite[:, None, :] * wide + total

    coeffs = expansion(chemical_potential[0], ORDER)
    probe_wide = probes.astype(jnp.float32)
    previous = probe_wide
    current = operate(probes)
    fermi_vec = coeffs[0] * previous + coeffs[1] * current
    for term_index in range(2, ORDER + 1):
        following = 2.0 * operate(current.astype(jnp.bfloat16)) - previous
        fermi_vec = fermi_vec + coeffs[term_index] * following
        previous, current = current, following

    norm_sq = jnp.sum(probe_wide * probe_wide, axis=(0, 2))
    scale = (NCLUS * BLOCK) / (norm_sq * PROBE_VECTORS)
    density = jnp.sum(probe_wide * fermi_vec * scale[None, :, None], axis=1)
    filling = jnp.sum(density).reshape(1) / (NCLUS * BLOCK)
    weighted = (fermi_vec * scale[None, :, None]).astype(jnp.bfloat16)
    weighted_wide = weighted.astype(jnp.float32)
    facing_all = jnp.transpose(bond_dir.astype(jnp.float32), (1, 0, 2))

    def force_slab(total, slab):
        blocks, gather_ids, targets, facing = slab
        blocks_wide = blocks.astype(jnp.float32)
        u_cols = jnp.take(weighted_wide, gather_ids, axis=0)
        v_cols = jnp.take(probe_wide, gather_ids, axis=0)
        dens = jnp.einsum("cpi,cpj->cij", weighted_wide, v_cols, precision=highest)
        dens = dens + jnp.einsum("cpi,cpj->cij", probe_wide, u_cols, precision=highest)
        product = dens * blocks_wide
        row_sums = jnp.sum(product, axis=2)
        col_sums = jnp.sum(product, axis=1)
        turned = facing.T
        row_terms = -DECAY * turned[:, :, None] * row_sums[:, None, :]
        col_terms = DECAY * turned[:, :, None] * col_sums[:, None, :]
        moved = jax.ops.segment_sum(col_terms, targets, num_segments=NCLUS + 1)[:NCLUS]
        return total + row_terms + moved, None

    orbital_gradient, unused = lax.scan(force_slab, jnp.zeros((NCLUS, 3, BLOCK), jnp.float32), (masked, safe_ids, target_ids, facing_all))
    atom_table = (atom_of[:, :, None] == jnp.arange(ATOMS, dtype=jnp.int32)[None, None, :]).astype(jnp.float32)
    forces = jnp.einsum("cxb,cba->xca", orbital_gradient, atom_table, precision=highest).reshape(3, NCLUS * ATOMS)
    return density, filling, forces
```

```python
import functools

import jax
import jax.numpy as jnp
import numpy as np
from jax import lax
from jax.experimental import pallas as pl
from jax.experimental.pallas import tpu as pltpu
from jax.sharding import PartitionSpec as P

MESH = pl.DeviceIdType.MESH
CL = 12
SLOTS = 20
ROWS = 16
B = 128
ATOMS = 32
REACH = 12
ORDER = 4
PROBE_VECTORS = 128
DECAY = 50.0
SMEARING_TEMP = 0.1
QUAD_NODES = 64
CHIPS_Y = 4
EMPTY = CL * SLOTS
F32 = jnp.float32
BF16 = jnp.bfloat16
FAR, NEAR = 0, 1
LINK = F32


def pair_offset(side, own, other):
    if side == FAR:
        return REACH - 1 - other - own if other + own <= REACH - 1 else None
    return 3 * REACH - 1 - other - own if other + own >= REACH - 1 else None


def kernel(
    clus, probe, probes_ref, onsite_ref, hop_ref, col_ref, atom_ref, bond_ref, mu_ref, cos_ref,
    density_ref, filling_ref, forces_ref,
    kbuf, ktbuf, tab_v, bond_v, tab, bond, xs, halo, part_out, part_in, cheb, fermi, y_acc, coef,
    norm_buf, norm_in, fill_buf, fill_in, dens_out, dens_in, wf, force_acc, col_out, col_in, onehot, z_out, z_in,
    ksem, tsem, hs, hr, ps, pr, ns, nr, gs, gr, ds, dr, fs, fr, zs, zr,
):
    me = lax.axis_index("clus")
    z = lax.axis_index("probe")
    flip = me % 2
    sign = 1 - 2 * flip
    place = [flip * (CL - 1) + sign * c for c in range(CL)]
    chip = me // 2
    cx, cy = chip // CHIPS_Y, chip % CHIPS_Y
    chips_x = clus // (2 * CHIPS_Y)

    far = ((me + clus - sign) % clus, z)
    near = (me + sign, z)
    y_peers = [((cx * CHIPS_Y + (cy + q) % CHIPS_Y) * 2 + flip, z) for q in range(1, CHIPS_Y)]
    x_peers = [((((cx + q) % chips_x) * CHIPS_Y + cy) * 2 + flip, z) for q in range(1, chips_x)]
    z_peers = [(me, (z + q) % probe) for q in range(1, probe)]

    def send(src, dst, s, r, peer):
        return pltpu.make_async_remote_copy(
            src_ref=src, dst_ref=dst, send_sem=s, recv_sem=r, device_id=peer, device_id_type=MESH
        )

    loads = [
        pltpu.make_async_copy(hop_ref.at[m], kbuf.at[pl.ds(m * CL, CL)], ksem.at[m]) for m in range(SLOTS)
    ]
    for copy in loads:
        copy.start()

    barrier = pltpu.get_barrier_semaphore()
    everyone = [far, near] + y_peers + x_peers + z_peers
    for peer in everyone:
        pl.semaphore_signal(barrier, inc=1, device_id=peer, device_id_type=MESH)

    lane = lax.broadcasted_iota(jnp.int32, (SLOTS, CL), 1)
    slot = lax.broadcasted_iota(jnp.int32, (SLOTS, CL), 0)
    columns = col_ref[...]
    rel = jnp.where(columns >= 0, columns - me * CL - lane + REACH, -1)
    rel = jnp.where(rel >= 0, rel * sign + flip * (2 * REACH), -1)
    flat = slot * CL + lane
    directions = [bond_ref[x].astype(F32) for x in range(3)]
    tab_v[...] = jnp.full(tab_v.shape, EMPTY, jnp.int32)
    bond_v[...] = jnp.zeros(bond_v.shape, F32)
    for o in range(2 * REACH + 1):
        hit = rel == o
        tab_v[o : o + 1, 0:CL] = jnp.min(jnp.where(hit, flat, EMPTY), axis=0, keepdims=True)
        for x in range(3):
            bond_v[x * 32 + o : x * 32 + o + 1, 0:CL] = jnp.sum(
                jnp.where(hit, directions[x], 0.0), axis=0, keepdims=True
            )
    tables = [pltpu.make_async_copy(tab_v, tab, tsem.at[0]), pltpu.make_async_copy(bond_v, bond, tsem.at[1])]
    for copy in tables:
        copy.start()

    nacc = jnp.zeros((ROWS, B), F32)
    for c in range(CL):
        xc = probes_ref[place[c]]
        xs[0, c] = xc
        wide = xc.astype(F32)
        cheb[0, c] = wide
        cheb[1, c] = jnp.zeros((ROWS, B), F32)
        nacc = nacc + wide * wide
    norm_buf[0] = nacc

    occupation = 1.0 / (1.0 + jnp.exp((cos_ref[1:2, :] - mu_ref[0]) / SMEARING_TEMP))
    weight = lax.broadcasted_iota(jnp.int32, (8, B), 0)
    total = jnp.sum(cos_ref[...] * occupation, axis=1, keepdims=True) * (2.0 / QUAD_NODES)
    coef[...] = jnp.broadcast_to(total, (8, B)) * jnp.where(weight == 0, 0.5, 1.0)
    for c in range(CL):
        fermi[c] = cheb[0, c] * coef[0:1, :]

    pl.semaphore_wait(barrier, len(everyone))

    def halo_copy(k, side):
        return send(xs.at[k], halo.at[k, side], hs.at[k, side], hr.at[k, side], (far, near)[side])

    def part_copy(k, side):
        return send(part_out.at[k, side], part_in.at[k, side], ps.at[k, side], pr.at[k, side], (far, near)[side])

    def stage_copies(own, arrived, s, r, stage, arriving=False):
        if stage == 0:
            return [send(own.at[0], arrived.at[0], s.at[0], r.at[0], near)]
        peers, first, count, at = ((y_peers, 1, CHIPS_Y, cy), (x_peers, 1 + CHIPS_Y, chips_x, cx))[stage - 1]
        copies = []
        for q, peer in enumerate(peers):
            slot = first + ((at + count - q - 1) % count if arriving else at)
            copies.append(send(own.at[stage], arrived.at[slot], s.at[first + q], r.at[slot], peer))
        return copies

    norm_copies = functools.partial(stage_copies, norm_buf, norm_in, ns, nr)
    fill_copies = functools.partial(stage_copies, fill_buf, fill_in, gs, gr)

    def collect(copies, own, arrived, stage):
        for copy in copies(stage, True):
            copy.wait_recv()
        if stage == 0:
            own[1] = own[0] + arrived[0]
            return
        first, count, at = ((1, CHIPS_Y, cy), (1 + CHIPS_Y, chips_x, cx))[stage - 1]
        arrived[first + at] = own[stage]
        value = arrived[first]
        for q in range(1, count):
            value = value + arrived[first + q]
        own[stage + 1] = value

    halo_copy(0, FAR).start()
    halo_copy(0, NEAR).start()
    for copy in norm_copies(0):
        copy.start()

    kbuf[EMPTY] = jnp.zeros((B, B), BF16)
    ktbuf[EMPTY] = jnp.zeros((B, B), BF16)

    def turn(m, carry):
        pltpu.make_async_copy(hop_ref.at[m], kbuf.at[pl.ds(m * CL, CL)], ksem.at[m]).wait()
        for c in range(CL):
            ktbuf[m * CL + c] = kbuf[m * CL + c].T
        return carry

    lax.fori_loop(0, SLOTS, turn, 0)
    for copy in tables:
        copy.wait()
    collect(norm_copies, norm_buf, norm_in, 0)
    for copy in norm_copies(1):
        copy.start()

    def straight(o, c):
        return kbuf[tab[o, place[c]]]

    def turned(o, c):
        return ktbuf[tab[o, place[c]]]

    def product(vectors, blocks):
        return jnp.dot(
            jnp.concatenate(vectors, axis=1), jnp.concatenate(blocks, axis=0), preferred_element_type=F32
        )

    def side_direct(k, side, c):
        others = [b for b in range(CL) if pair_offset(side, c, b) is not None]
        return product(
            [halo[k, side, b] for b in others], [turned(pair_offset(side, c, b), c) for b in others]
        )

    def apply(k, carry):
        @pl.when(k >= 1)
        def _():
            halo_copy(k, FAR).start()
            halo_copy(k, NEAR).start()

        x = [xs[k, c] for c in range(CL)]
        for side in (FAR, NEAR):
            for b in range(CL):
                own = [c for c in range(CL) if pair_offset(side, c, b) is not None]
                part_out[k, side, b] = product(
                    [x[c] for c in own], [straight(pair_offset(side, c, b), c) for c in own]
                ).astype(LINK)
            part_copy(k, side).start()
        for c in range(CL):
            y_acc[c] = product(
                x + x,
                [turned(REACH + d - c, c) for d in range(CL)] + [straight(REACH + c - d, d) for d in range(CL)],
            )

        @pl.when(k == 1)
        def _():
            collect(norm_copies, norm_buf, norm_in, 1)
            for copy in norm_copies(2):
                copy.start()

        halo_copy(k, NEAR).wait_recv()
        for c in range(CL):
            y_acc[c] = y_acc[c] + side_direct(k, NEAR, c)
        halo_copy(k, FAR).wait_recv()
        for c in range(CL):
            y_acc[c] = y_acc[c] + side_direct(k, FAR, c)
        part_copy(k, NEAR).wait_recv()
        part_copy(k, FAR).wait_recv()
        alpha = jnp.where(k == 0, 1.0, 2.0)
        into = (k + 1) % 2
        for c in range(CL):
            image = y_acc[c] + part_in[k, NEAR, c].astype(F32) + part_in[k, FAR, c].astype(F32)
            image = image + onsite_ref[pl.ds(place[c], 1), :] * xs[k, c].astype(F32)
            following = alpha * image - cheb[into, c]
            cheb[into, c] = following
            fermi[c] = fermi[c] + coef[pl.ds(k + 1, 1), :] * following
            xs[k + 1, c] = following.astype(BF16)
        return carry

    lax.fori_loop(0, ORDER, apply, 0)

    collect(norm_copies, norm_buf, norm_in, 2)
    norm_sq = jnp.sum(norm_buf[3], axis=1, keepdims=True)
    scale = jnp.broadcast_to((clus * CL * B) / (norm_sq * PROBE_VECTORS), (ROWS, B))
    for c in range(CL):
        scaled = fermi[c] * scale
        fermi[c] = scaled
        xs[ORDER, c] = scaled.astype(BF16)
    halo_copy(ORDER, FAR).start()
    halo_copy(ORDER, NEAR).start()
    filled = jnp.zeros((1, B), F32)
    dens_out[...] = jnp.zeros(dens_out.shape, F32)
    for c in range(CL):
        row = jnp.sum(xs[0, c].astype(F32) * fermi[c], axis=0, keepdims=True)
        dens_out[c : c + 1, :] = row
        filled = filled + row
        wf[c] = xs[ORDER, c].astype(F32)
    fill_buf[0] = jnp.broadcast_to(filled, (8, B))

    def z_copies(src, dst, s, r, arriving=False):
        copies = []
        for q, peer in enumerate(z_peers):
            slot = (z + probe - q - 1) % probe if arriving else z
            copies.append(send(src, dst.at[slot], s.at[q], r.at[slot], peer))
        return copies

    def z_sum(src, dst, s, r):
        dst[z] = src[...]
        for copy in z_copies(src, dst, s, r, True):
            copy.wait_recv()
        value = dst[0]
        for q in range(1, probe):
            value = value + dst[q]
        return value

    for copy in fill_copies(0):
        copy.start()
    for copy in z_copies(dens_out, dens_in, ds, dr):
        copy.start()

    def sums(left, block, u, v):
        image = jnp.dot(left, block, preferred_element_type=F32)
        r = v * image[:ROWS] + u * image[ROWS:]
        return r[:8] + r[8:]

    both = [jnp.concatenate([xs[0, c], xs[ORDER, c]], axis=0) for c in range(CL)]

    def own_vectors(c):
        return xs[0, c].astype(F32), xs[ORDER, c].astype(F32)

    def add(acc, o, c, r, positive):
        out = []
        for x in range(3):
            term = bond[x * 32 + o, place[c]] * r
            out.append(acc[x] + term if positive else acc[x] - term)
        return out

    zero3 = [jnp.zeros((8, B), F32)] * 3
    for c in range(CL):
        u, v = own_vectors(c)
        acc = zero3
        for d in range(CL):
            o = REACH + d - c
            acc = add(acc, o, c, sums(both[d], turned(o, c), u, v), False)
        for d in range(CL):
            o = REACH + c - d
            acc = add(acc, o, d, sums(both[d], straight(o, d), u, v), True)
        for x in range(3):
            force_acc[c, x] = acc[x]

    collect(fill_copies, fill_buf, fill_in, 0)
    for copy in fill_copies(1):
        copy.start()

    def col_copy(side):
        return send(col_out.at[side], col_in.at[side], fs.at[side], fr.at[side], (far, near)[side])

    def halo_both(side, b):
        return jnp.concatenate([halo[0, side, b], halo[ORDER, side, b]], axis=0)

    for side in (NEAR, FAR):
        halo_copy(ORDER, side).wait_recv()
        for b in range(CL):
            u, v = halo[0, side, b].astype(F32), halo[ORDER, side, b].astype(F32)
            acc = zero3
            for c in range(CL):
                o = pair_offset(side, c, b)
                if o is not None:
                    acc = add(acc, o, c, sums(both[c], straight(o, c), u, v), True)
            for x in range(3):
                col_out[side, 3 * b + x : 3 * b + x + 1, :] = jnp.sum(acc[x], axis=0, keepdims=True)
        col_copy(side).start()
        for c in range(CL):
            u, v = own_vectors(c)
            acc = [force_acc[c, x] for x in range(3)]
            for b in range(CL):
                o = pair_offset(side, c, b)
                if o is not None:
                    acc = add(acc, o, c, sums(halo_both(side, b), turned(o, c), u, v), False)
            for x in range(3):
                force_acc[c, x] = acc[x]

    collect(fill_copies, fill_buf, fill_in, 1)
    for copy in fill_copies(2):
        copy.start()

    row = lax.broadcasted_iota(jnp.int32, (B, B), 0)
    for c in range(CL):
        owner = atom_ref[c : c + 1, :] + ATOMS * (c % 4)
        onehot[c] = (row == owner).astype(BF16)

    summed = z_sum(dens_out, dens_in, ds, dr)
    for c in range(CL):
        density_ref[pl.ds(place[c], 1), :] = summed[c : c + 1, :]

    for side in (NEAR, FAR):
        col_copy(side).wait_recv()
    for c in range(CL):
        for x in range(3):
            j = 3 * c + x
            value = jnp.sum(force_acc[c, x], axis=0, keepdims=True)
            value = value + col_in[NEAR, j : j + 1, :] + col_in[FAR, j : j + 1, :]
            force_acc[c, x] = jnp.broadcast_to(value * DECAY, (8, B))

    dims = (((1,), (1,)), ((), ()))
    z_out[...] = jnp.zeros(z_out.shape, F32)
    pick = lax.broadcasted_iota(jnp.int32, (8, B), 0)
    for quad in range(CL // 4):
        total = jnp.zeros((8, B), F32)
        for i in range(4):
            c = quad * 4 + i
            there = place[c]
            value = jnp.where(
                pick == 0, force_acc[there, 0], jnp.where(pick == 1, force_acc[there, 1], force_acc[there, 2])
            )
            high = value.astype(BF16)
            rest = value - high.astype(F32)
            middle = rest.astype(BF16)
            low = (rest - middle.astype(F32)).astype(BF16)
            for piece in (high, middle, low):
                total = total + lax.dot_general(piece, onehot[c], dims, preferred_element_type=F32)
        z_out[pl.ds(quad * 3, 3), :] = total[0:3]
    collect(fill_copies, fill_buf, fill_in, 2)
    z_out[9:10, :] = fill_buf[3, 0:1, :]
    for copy in z_copies(z_out, z_in, zs, zr):
        copy.start()
    summed = z_sum(z_out, z_in, zs, zr)
    for quad in range(CL // 4):
        forces_ref[:, quad * B : (quad + 1) * B] = summed[quad * 3 : quad * 3 + 3]
    filling_ref[0] = jnp.sum(summed[9:10, :]) / (clus * CL * B)

    def finish(k, carry):
        for side in (FAR, NEAR):
            halo_copy(k, side).wait_send()
            part_copy(k, side).wait_send()
        return carry

    lax.fori_loop(0, ORDER, finish, 0)
    for side in (FAR, NEAR):
        halo_copy(ORDER, side).wait_send()
        col_copy(side).wait_send()
    for stage in range(3):
        for copy in norm_copies(stage) + fill_copies(stage):
            copy.wait_send()
    for copy in z_copies(dens_out, dens_in, ds, dr) + z_copies(z_out, z_in, zs, zr):
        copy.wait_send()


def cosines():
    angles = np.pi * (np.arange(QUAD_NODES) + 0.5) / QUAD_NODES
    table = np.zeros((8, B), np.float32)
    for k in range(ORDER + 1):
        table[k, :QUAD_NODES] = np.cos(k * angles)
    return table


def solution(mesh):
    clus, probe = mesh.shape["clus"], mesh.shape["probe"]
    small = 1 + CHIPS_Y + clus // (2 * CHIPS_Y)
    vmem, dma = pltpu.VMEM, pltpu.SemaphoreType.DMA

    def local(probes, onsite, hopping, block_col, atom_of, bond_dir, chemical_potential):
        in_vmem = pl.BlockSpec(memory_space=pltpu.VMEM)
        in_smem = pl.BlockSpec(memory_space=pltpu.SMEM)
        in_hbm = pl.BlockSpec(memory_space=pltpu.HBM)
        return pl.pallas_call(
            functools.partial(kernel, clus, probe),
            out_shape=(
                jax.ShapeDtypeStruct((CL, B), F32),
                jax.ShapeDtypeStruct((1,), F32),
                jax.ShapeDtypeStruct((3, CL * ATOMS), F32),
            ),
            in_specs=[in_vmem, in_vmem, in_hbm, in_vmem, in_vmem, in_vmem, in_smem, in_vmem],
            out_specs=(in_vmem, in_smem, in_vmem),
            scratch_shapes=[
                vmem((EMPTY + 1, B, B), BF16),
                vmem((EMPTY + 1, B, B), BF16),
                vmem((32, B), jnp.int32),
                vmem((96, B), F32),
                pltpu.SMEM((32, B), jnp.int32),
                pltpu.SMEM((96, B), F32),
                vmem((ORDER + 1, CL, ROWS, B), BF16),
                vmem((ORDER + 1, 2, CL, ROWS, B), BF16),
                vmem((ORDER, 2, CL, ROWS, B), LINK),
                vmem((ORDER, 2, CL, ROWS, B), LINK),
                vmem((2, CL, ROWS, B), F32),
                vmem((CL, ROWS, B), F32),
                vmem((CL, ROWS, B), F32),
                vmem((8, B), F32),
                vmem((4, ROWS, B), F32),
                vmem((small, ROWS, B), F32),
                vmem((4, 8, B), F32),
                vmem((small, 8, B), F32),
                vmem((16, B), F32),
                vmem((probe, 16, B), F32),
                vmem((CL, ROWS, B), F32),
                vmem((CL, 3, 8, B), F32),
                vmem((2, 40, B), F32),
                vmem((2, 40, B), F32),
                vmem((CL, B, B), BF16),
                vmem((16, B), F32),
                vmem((probe, 16, B), F32),
                dma((SLOTS,)),
                dma((2,)),
                dma((ORDER + 1, 2)),
                dma((ORDER + 1, 2)),
                dma((ORDER, 2)),
                dma((ORDER, 2)),
                dma((small,)),
                dma((small,)),
                dma((small,)),
                dma((small,)),
                dma((probe,)),
                dma((probe,)),
                dma((2,)),
                dma((2,)),
                dma((probe,)),
                dma((probe,)),
            ],
            compiler_params=pltpu.CompilerParams(
                collective_id=0, has_side_effects=True, vmem_limit_bytes=40 * 1024 * 1024
            ),
            cost_estimate=pl.CostEstimate(flops=2_600_000_000, bytes_accessed=8_500_000, transcendentals=0),
            name="fermi_forces",
        )(probes, onsite, hopping, block_col, atom_of, bond_dir, chemical_potential, jnp.asarray(cosines()))

    return jax.shard_map(
        local,
        mesh=mesh,
        in_specs=(
            P("clus", "probe", None),
            P("clus", None),
            P(None, "clus", None, None),
            P(None, "clus"),
            P("clus", None),
            P(None, None, "clus"),
            P(),
        ),
        out_specs=(P("clus", None), P(), P(None, "clus")),
        check_vma=False,
    )
```

```python
import functools

import jax
import jax.numpy as jnp
import numpy as np
from jax import lax
from jax.experimental import pallas as pl
from jax.experimental.pallas import tpu as pltpu
from jax.sharding import PartitionSpec as P

MESH = pl.DeviceIdType.MESH
CL = 12
SLOTS = 20
ROWS = 16
B = 128
ATOMS = 32
REACH = 12
ORDER = 4
PROBE_VECTORS = 128
DECAY = 50.0
SMEARING_TEMP = 0.1
QUAD_NODES = 64
EMPTY = CL * SLOTS
F32 = jnp.float32
BF16 = jnp.bfloat16
FAR, NEAR = 0, 1
LINK = BF16


def pair_offset(side, own, other):
    if side == FAR:
        return REACH - 1 - other - own if other + own <= REACH - 1 else None
    return 3 * REACH - 1 - other - own if other + own >= REACH - 1 else None


def kernel(
    clus, probe, probes_hbm, onsite_hbm, hop_ref, col_hbm, atom_hbm, bond_hbm, mu_hbm, cos_hbm,
    density_hbm, filling_hbm, forces_hbm,
    density_ref, filling_ref, forces_ref, mu_ref, probes_ref, onsite_ref, col_ref, atom_ref, bond_ref, cos_ref, atom_far, kbuf, ktbuf, tab_v, bond_v, tab, bond, xs, halo, part_out, part_in, cheb, fermi, y_acc, coef,
    norm_buf, norm_in, fill_buf, fill_in, dens_out, dens_in, force_acc, far_acc, col_out, col_in, onehot, z_out, z_in, f_out, f_in,
    isem, osem, ksem, tsem, asem, hs, hr, ps, pr, ns, nr, gs, gr, ds, dr, fs, fr, zs, zr, ws, wr,
):
    me = lax.axis_index("clus")
    z = lax.axis_index("probe")
    flip = me % 2
    sign = 1 - 2 * flip
    place = [flip * (CL - 1) + sign * c for c in range(CL)]
    chips = clus // 2
    chip = me // 2
    has_far = jnp.logical_and(me > 0, me < clus - 1)

    far_clus = (me + clus - sign) % clus
    far = (far_clus, z)
    near = (me + sign, z)
    chip_peers = [(((chip + q) % chips) * 2 + flip, z) for q in range(1, chips)]
    z_peers = [(me, (z + q) % probe) for q in range(1, probe)]
    far_peers = [(far_clus, (z + q) % probe) for q in range(probe)]

    barrier = pltpu.get_barrier_semaphore()
    everyone = [near] + chip_peers + z_peers
    for peer in everyone:
        pl.semaphore_signal(barrier, inc=1, device_id=peer, device_id_type=MESH)

    @pl.when(has_far)
    def _():
        for peer in far_peers:
            pl.semaphore_signal(barrier, inc=1, device_id=peer, device_id_type=MESH)

    def send(src, dst, s, r, peer):
        return pltpu.make_async_remote_copy(
            src_ref=src, dst_ref=dst, send_sem=s, recv_sem=r, device_id=peer, device_id_type=MESH
        )

    loads = [
        pltpu.make_async_copy(hop_ref.at[m], kbuf.at[pl.ds(m * CL, CL)], ksem.at[m]) for m in range(SLOTS)
    ]
    inputs = [
        pltpu.make_async_copy(source, target, isem.at[i])
        for i, (source, target) in enumerate(
            (
                (col_hbm, col_ref), (bond_hbm, bond_ref), (probes_hbm, probes_ref), (cos_hbm, cos_ref),
                (atom_hbm, atom_ref), (onsite_hbm, onsite_ref), (mu_hbm, mu_ref),
            )
        )
    ]
    for copy in inputs + loads:
        copy.start()
    for copy in inputs:
        copy.wait()

    lane = lax.broadcasted_iota(jnp.int32, (CL, SLOTS), 0)
    slot = lax.broadcasted_iota(jnp.int32, (CL, SLOTS), 1)
    columns = col_ref[...]
    rel = jnp.where(columns >= 0, columns - me * CL - lane + REACH, -1)
    rel = jnp.where(rel >= 0, rel * sign + flip * (2 * REACH), -1)
    flat = slot * CL + lane
    directions = [bond_ref[x].astype(F32) for x in range(3)]
    wide_lane = lax.broadcasted_iota(jnp.int32, (CL, B), 1)
    places = jnp.full((CL, B), EMPTY, jnp.int32)
    facing = [jnp.zeros((CL, B), F32)] * 3
    for o in range(2 * REACH + 1):
        hit = rel == o
        here = wide_lane == o
        places = jnp.where(here, jnp.min(jnp.where(hit, flat, EMPTY), axis=1, keepdims=True), places)
        for x in range(3):
            facing[x] = jnp.where(
                here, jnp.sum(jnp.where(hit, directions[x], 0.0), axis=1, keepdims=True), facing[x]
            )
    tab_v[0:CL, :] = places
    for x in range(3):
        bond_v[16 * x : 16 * x + CL, :] = facing[x]
    tables = [pltpu.make_async_copy(tab_v, tab, tsem.at[0]), pltpu.make_async_copy(bond_v, bond, tsem.at[1])]
    for copy in tables:
        copy.start()

    @pl.when(jnp.logical_not(has_far))
    def _():
        f_in[...] = jnp.zeros(f_in.shape, F32)
        atom_far[...] = jnp.zeros(atom_far.shape, jnp.int32)
        halo[:, FAR] = jnp.zeros((ORDER + 1, CL, ROWS, B), BF16)
        part_in[:, FAR] = jnp.zeros((ORDER, CL, ROWS, B), LINK)

    nacc = jnp.zeros((ROWS, B), F32)
    for c in range(CL):
        xc = probes_ref[place[c]]
        xs[0, c] = xc
        wide = xc.astype(F32)
        cheb[0, c] = wide
        cheb[1, c] = jnp.zeros((ROWS, B), F32)
        nacc = nacc + wide * wide
    norm_buf[0] = nacc

    occupation = 1.0 / (1.0 + jnp.exp((cos_ref[1:2, :] - mu_ref[0]) / SMEARING_TEMP))
    weight = lax.broadcasted_iota(jnp.int32, (8, B), 0)
    total = jnp.sum(cos_ref[...] * occupation, axis=1, keepdims=True) * (2.0 / QUAD_NODES)
    coef[...] = jnp.broadcast_to(total, (8, B)) * jnp.where(weight == 0, 0.5, 1.0)
    for c in range(CL):
        fermi[c] = cheb[0, c] * coef[0:1, :]

    pl.semaphore_wait(barrier, len(everyone) + len(far_peers) * has_far.astype(jnp.int32))

    def halo_copy(k, side):
        return send(xs.at[k], halo.at[k, side], hs.at[k, side], hr.at[k, side], (far, near)[side])

    def part_copy(k, side):
        return send(part_out.at[k, side], part_in.at[k, side], ps.at[k, side], pr.at[k, side], (far, near)[side])

    def stage_copies(own, arrived, s, r, stage, arriving=False):
        if stage == 0:
            return [send(own.at[0], arrived.at[chips], s.at[0], r.at[chips], near)]
        copies = []
        for q, peer in enumerate(chip_peers):
            place_in = (chip + chips - q - 1) % chips if arriving else chip
            copies.append(send(own.at[stage], arrived.at[place_in], s.at[1 + q], r.at[place_in], peer))
        return copies

    norm_copies = functools.partial(stage_copies, norm_buf, norm_in, ns, nr)
    fill_copies = functools.partial(stage_copies, fill_buf, fill_in, gs, gr)

    def collect(copies, own, arrived, stage):
        for copy in copies(stage, True):
            copy.wait_recv()
        if stage == 0:
            own[1] = own[0] + arrived[chips]
            return
        arrived[chip] = own[stage]
        value = arrived[0]
        for q in range(1, chips):
            value = value + arrived[q]
        own[stage + 1] = value

    def atoms_copy():
        return send(atom_ref, atom_far, asem.at[0], asem.at[1], far)

    @pl.when(has_far)
    def _():
        halo_copy(0, FAR).start()
        atoms_copy().start()

    halo_copy(0, NEAR).start()
    for copy in norm_copies(0):
        copy.start()

    kbuf[EMPTY] = jnp.zeros((B, B), BF16)
    ktbuf[EMPTY] = jnp.zeros((B, B), BF16)

    def turn(m, carry):
        pltpu.make_async_copy(hop_ref.at[m], kbuf.at[pl.ds(m * CL, CL)], ksem.at[m]).wait()
        for c in range(CL):
            ktbuf[m * CL + c] = kbuf[m * CL + c].T
        return carry

    lax.fori_loop(0, SLOTS, turn, 0)
    for copy in tables:
        copy.wait()
    collect(norm_copies, norm_buf, norm_in, 0)
    for copy in norm_copies(1):
        copy.start()

    def straight(o, c):
        return kbuf[tab[place[c], o]]

    def turned(o, c):
        return ktbuf[tab[place[c], o]]

    def product(vectors, blocks):
        return jnp.dot(
            jnp.concatenate(vectors, axis=1), jnp.concatenate(blocks, axis=0), preferred_element_type=F32
        )

    def side_direct(k, side, c):
        others = [b for b in range(CL) if pair_offset(side, c, b) is not None]
        return product(
            [halo[k, side, b] for b in others], [turned(pair_offset(side, c, b), c) for b in others]
        )

    def apply(k, carry):
        @pl.when(jnp.logical_and(k >= 1, has_far))
        def _():
            halo_copy(k, FAR).start()

        @pl.when(k >= 1)
        def _():
            halo_copy(k, NEAR).start()

        x = [xs[k, c] for c in range(CL)]
        for side in (FAR, NEAR):
            for b in range(CL):
                own = [c for c in range(CL) if pair_offset(side, c, b) is not None]
                part_out[k, side, b] = product(
                    [x[c] for c in own], [straight(pair_offset(side, c, b), c) for c in own]
                ).astype(LINK)
            if side == FAR:

                @pl.when(has_far)
                def _():
                    part_copy(k, FAR).start()

            else:
                part_copy(k, NEAR).start()
        for c in range(CL):
            y_acc[c] = product(
                x + x,
                [turned(REACH + d - c, c) for d in range(CL)] + [straight(REACH + c - d, d) for d in range(CL)],
            )

        @pl.when(k == 2)
        def _():
            collect(norm_copies, norm_buf, norm_in, 1)
            norm_sq = jnp.sum(norm_buf[2], axis=1, keepdims=True)
            norm_buf[3] = jnp.broadcast_to((clus * CL * B) / (norm_sq * PROBE_VECTORS), (ROWS, B))

        halo_copy(k, NEAR).wait_recv()
        for c in range(CL):
            y_acc[c] = y_acc[c] + side_direct(k, NEAR, c)
        part_copy(k, NEAR).wait_recv()

        @pl.when(has_far)
        def _():
            halo_copy(k, FAR).wait_recv()

        for c in range(CL):
            y_acc[c] = y_acc[c] + part_in[k, NEAR, c].astype(F32) + side_direct(k, FAR, c)

        @pl.when(has_far)
        def _():
            part_copy(k, FAR).wait_recv()

        alpha = jnp.where(k == 0, 1.0, 2.0)
        into = (k + 1) % 2
        for c in range(CL):
            image = y_acc[c] + part_in[k, FAR, c].astype(F32)
            image = image + onsite_ref[pl.ds(place[c], 1), :] * xs[k, c].astype(F32)
            following = alpha * image - cheb[into, c]
            cheb[into, c] = following
            fermi[c] = fermi[c] + coef[pl.ds(k + 1, 1), :] * following
            xs[k + 1, c] = following.astype(BF16)
        return carry

    lax.fori_loop(0, ORDER, apply, 0)

    scale = norm_buf[3]
    for c in range(CL):
        scaled = fermi[c] * scale
        fermi[c] = scaled
        xs[ORDER, c] = scaled.astype(BF16)

    @pl.when(has_far)
    def _():
        halo_copy(ORDER, FAR).start()

    halo_copy(ORDER, NEAR).start()
    filled = jnp.zeros((1, B), F32)
    dens_out[...] = jnp.zeros(dens_out.shape, F32)
    for c in range(CL):
        row = jnp.sum(xs[0, c].astype(F32) * fermi[c], axis=0, keepdims=True)
        dens_out[c : c + 1, :] = row
        filled = filled + row
    fill_buf[0] = jnp.broadcast_to(filled, (8, B))

    def z_copies(src, dst, s, r, arriving=False):
        copies = []
        for q, peer in enumerate(z_peers):
            slot = (z + probe - q - 1) % probe if arriving else z
            copies.append(send(src, dst.at[slot], s.at[q], r.at[slot], peer))
        return copies

    def z_sum(src, dst, s, r):
        dst[z] = src[...]
        for copy in z_copies(src, dst, s, r, True):
            copy.wait_recv()
        value = dst[0]
        for q in range(1, probe):
            value = value + dst[q]
        return value

    for copy in fill_copies(0):
        copy.start()
    for copy in z_copies(dens_out, dens_in, ds, dr):
        copy.start()

    def sums(left, block, u, v):
        image = jnp.dot(left, block, preferred_element_type=F32)
        r = v * image[:ROWS] + u * image[ROWS:]
        return r[:8] + r[8:]

    both = [jnp.concatenate([xs[0, c], xs[ORDER, c]], axis=0) for c in range(CL)]

    def own_vectors(c):
        return xs[0, c].astype(F32), xs[ORDER, c].astype(F32)

    def add(acc, o, c, r, positive):
        out = []
        for x in range(3):
            term = bond[16 * x + place[c], o] * r
            out.append(acc[x] + term if positive else acc[x] - term)
        return out

    zero3 = [jnp.zeros((8, B), F32)] * 3
    for c in range(CL):
        if c == CL // 3:
            collect(fill_copies, fill_buf, fill_in, 0)
            for copy in fill_copies(1):
                copy.start()
        u, v = own_vectors(c)
        acc = zero3
        for d in range(CL):
            o = REACH + d - c
            acc = add(acc, o, c, sums(both[d], turned(o, c), u, v), False)
        for d in range(CL):
            o = REACH + c - d
            acc = add(acc, o, d, sums(both[d], straight(o, d), u, v), True)
        for x in range(3):
            force_acc[c, x] = acc[x]

    def col_copy():
        return send(col_out, col_in, fs.at[0], fr.at[0], near)

    row = lax.broadcasted_iota(jnp.int32, (B, B), 0)

    @pl.when(has_far)
    def _():
        atoms_copy().wait_recv()

    for c in range(CL):
        onehot[0, c] = (row == atom_ref[c : c + 1, :] + ATOMS * (c % 4)).astype(BF16)
        onehot[1, c] = (row == atom_far[c : c + 1, :] + ATOMS * (c % 4)).astype(BF16)

    dims = (((1,), (1,)), ((), ()))
    pick = lax.broadcasted_iota(jnp.int32, (8, B), 0)

    def atom_sums(which, source, target):
        for quad in range(CL // 4):
            total = jnp.zeros((8, B), F32)
            for c in range(quad * 4, quad * 4 + 4):
                value = jnp.where(pick == 0, source(c, 0), jnp.where(pick == 1, source(c, 1), source(c, 2)))
                high = value.astype(BF16)
                rest = value - high.astype(F32)
                middle = rest.astype(BF16)
                low = (rest - middle.astype(F32)).astype(BF16)
                for piece in (high, middle, low):
                    total = total + lax.dot_general(piece, onehot[which, c], dims, preferred_element_type=F32)
            target[quad * 3 : quad * 3 + 3, :] = total[0:3]

    def far_copies(arriving=False):
        copies = []
        for q, peer in enumerate(far_peers):
            place_in = (z + probe - q) % probe if arriving else z
            copies.append(send(f_out, f_in.at[place_in], ws.at[q], wr.at[place_in], peer))
        return copies

    def halo_both(side, b):
        return jnp.concatenate([halo[0, side, b], halo[ORDER, side, b]], axis=0)

    z_out[...] = jnp.zeros(z_out.shape, F32)
    f_out[...] = jnp.zeros(f_out.shape, F32)
    for side in (NEAR, FAR):
        if side == NEAR:
            halo_copy(ORDER, NEAR).wait_recv()
        else:

            @pl.when(has_far)
            def _():
                halo_copy(ORDER, FAR).wait_recv()

        for b in range(CL):
            u, v = halo[0, side, b].astype(F32), halo[ORDER, side, b].astype(F32)
            acc = zero3
            for c in range(CL):
                o = pair_offset(side, c, b)
                if o is not None:
                    acc = add(acc, o, c, sums(both[c], straight(o, c), u, v), True)
            for x in range(3):
                total = jnp.sum(acc[x], axis=0, keepdims=True)
                if side == NEAR:
                    col_out[3 * b + x : 3 * b + x + 1, :] = total
                else:
                    far_acc[b, x] = jnp.broadcast_to(total * DECAY, (8, B))
        if side == NEAR:
            col_copy().start()
        else:
            atom_sums(1, lambda c, x: far_acc[(1 - flip) * (CL - 1) - sign * c, x], f_out)

            @pl.when(has_far)
            def _():
                for copy in far_copies():
                    copy.start()

        for c in range(CL):
            u, v = own_vectors(c)
            acc = [force_acc[c, x] for x in range(3)]
            for b in range(CL):
                o = pair_offset(side, c, b)
                if o is not None:
                    acc = add(acc, o, c, sums(halo_both(side, b), turned(o, c), u, v), False)
            for x in range(3):
                force_acc[c, x] = acc[x]

    col_copy().wait_recv()
    for c in range(CL):
        for x in range(3):
            j = 3 * c + x
            value = jnp.sum(force_acc[c, x], axis=0, keepdims=True) + col_in[j : j + 1, :]
            force_acc[c, x] = jnp.broadcast_to(value * DECAY, (8, B))
    atom_sums(0, lambda c, x: force_acc[place[c], x], z_out)
    collect(fill_copies, fill_buf, fill_in, 1)
    z_out[9:10, :] = fill_buf[2, 0:1, :]
    for copy in z_copies(z_out, z_in, zs, zr):
        copy.start()

    summed = z_sum(dens_out, dens_in, ds, dr)
    for c in range(CL):
        density_ref[pl.ds(place[c], 1), :] = summed[c : c + 1, :]
    results = [
        pltpu.make_async_copy(source, target, osem.at[i])
        for i, (source, target) in enumerate(
            ((density_ref, density_hbm), (forces_ref, forces_hbm), (filling_ref, filling_hbm))
        )
    ]
    results[0].start()

    @pl.when(has_far)
    def _():
        for copy in far_copies(True):
            copy.wait_recv()

    summed = z_sum(z_out, z_in, zs, zr)
    for q in range(probe):
        summed = summed + f_in[q]
    for quad in range(CL // 4):
        forces_ref[:, quad * B : (quad + 1) * B] = summed[quad * 3 : quad * 3 + 3]
    results[1].start()
    filling_ref[0] = jnp.sum(summed[9:10, :]) / (clus * CL * B)
    results[2].start()

    def finish(k, carry):
        halo_copy(k, NEAR).wait_send()
        part_copy(k, NEAR).wait_send()

        @pl.when(has_far)
        def _():
            halo_copy(k, FAR).wait_send()
            part_copy(k, FAR).wait_send()

        return carry

    lax.fori_loop(0, ORDER, finish, 0)
    halo_copy(ORDER, NEAR).wait_send()
    col_copy().wait_send()

    @pl.when(has_far)
    def _():
        halo_copy(ORDER, FAR).wait_send()
        atoms_copy().wait_send()
        for copy in far_copies():
            copy.wait_send()

    for stage in range(2):
        for copy in norm_copies(stage) + fill_copies(stage):
            copy.wait_send()
    for copy in z_copies(dens_out, dens_in, ds, dr) + z_copies(z_out, z_in, zs, zr):
        copy.wait_send()
    for copy in results:
        copy.wait()


def hand_over(density, filling, forces, density_out, filling_out, forces_out, sems):
    copies = [
        pltpu.make_async_copy(source, target, sems.at[i])
        for i, (source, target) in enumerate(((density, density_out), (filling, filling_out), (forces, forces_out)))
    ]
    for copy in copies:
        copy.start()
    for copy in copies:
        copy.wait()


def cosines():
    angles = np.pi * (np.arange(QUAD_NODES) + 0.5) / QUAD_NODES
    table = np.zeros((8, B), np.float32)
    for k in range(ORDER + 1):
        table[k, :QUAD_NODES] = np.cos(k * angles)
    return table


def solution(mesh):
    clus, probe = mesh.shape["clus"], mesh.shape["probe"]
    small = 1 + clus // 2
    vmem, dma = pltpu.VMEM, pltpu.SemaphoreType.DMA

    def local(probes, onsite, hopping, block_col, atom_of, bond_dir, chemical_potential):
        in_hbm = pl.BlockSpec(memory_space=pltpu.HBM)
        shapes = (
            jax.ShapeDtypeStruct((CL, B), F32),
            jax.ShapeDtypeStruct((1,), F32),
            jax.ShapeDtypeStruct((3, CL * ATOMS), F32),
        )
        found = pl.pallas_call(
            functools.partial(kernel, clus, probe),
            out_shape=shapes,
            in_specs=[in_hbm] * 8,
            out_specs=(in_hbm,) * 3,
            scratch_shapes=[
                vmem((CL, B), F32),
                pltpu.SMEM((1,), F32),
                vmem((3, CL * ATOMS), F32),
                pltpu.SMEM((1,), F32),
                vmem((CL, ROWS, B), BF16),
                vmem((CL, B), F32),
                vmem((CL, SLOTS), jnp.int32),
                vmem((CL, B), jnp.int32),
                vmem((3, CL, SLOTS), BF16),
                vmem((8, B), F32),
                vmem((CL, B), jnp.int32),
                vmem((EMPTY + 1, B, B), BF16),
                vmem((EMPTY + 1, B, B), BF16),
                vmem((16, B), jnp.int32),
                vmem((48, B), F32),
                pltpu.SMEM((16, B), jnp.int32),
                pltpu.SMEM((48, B), F32),
                vmem((ORDER + 1, CL, ROWS, B), BF16),
                vmem((ORDER + 1, 2, CL, ROWS, B), BF16),
                vmem((ORDER, 2, CL, ROWS, B), LINK),
                vmem((ORDER, 2, CL, ROWS, B), LINK),
                vmem((2, CL, ROWS, B), F32),
                vmem((CL, ROWS, B), F32),
                vmem((CL, ROWS, B), F32),
                vmem((8, B), F32),
                vmem((4, ROWS, B), F32),
                vmem((small, ROWS, B), F32),
                vmem((4, 8, B), F32),
                vmem((small, 8, B), F32),
                vmem((16, B), F32),
                vmem((probe, 16, B), F32),
                vmem((CL, 3, 8, B), F32),
                vmem((CL, 3, 8, B), F32),
                vmem((40, B), F32),
                vmem((40, B), F32),
                vmem((2, CL, B, B), BF16),
                vmem((16, B), F32),
                vmem((probe, 16, B), F32),
                vmem((16, B), F32),
                vmem((probe, 16, B), F32),
                dma((7,)),
                dma((3,)),
                dma((SLOTS,)),
                dma((2,)),
                dma((2,)),
                dma((ORDER + 1, 2)),
                dma((ORDER + 1, 2)),
                dma((ORDER, 2)),
                dma((ORDER, 2)),
                dma((small,)),
                dma((small,)),
                dma((small,)),
                dma((small,)),
                dma((probe,)),
                dma((probe,)),
                dma((1,)),
                dma((1,)),
                dma((probe,)),
                dma((probe,)),
                dma((probe,)),
                dma((probe,)),
            ],
            compiler_params=pltpu.CompilerParams(
                collective_id=0, has_side_effects=True, vmem_limit_bytes=60 * 1024 * 1024
            ),
            cost_estimate=pl.CostEstimate(flops=2_600_000_000, bytes_accessed=8_500_000, transcendentals=0),
            name="fermi_forces",
        )(
            probes, onsite, hopping, block_col.T, atom_of, jnp.swapaxes(bond_dir, 1, 2), chemical_potential,
            jnp.asarray(cosines()),
        )
        return pl.pallas_call(
            hand_over,
            out_shape=shapes,
            in_specs=[in_hbm] * 3,
            out_specs=(in_hbm,) * 3,
            scratch_shapes=[dma((3,))],
            compiler_params=pltpu.CompilerParams(vmem_limit_bytes=60 * 1024 * 1024),
            name="hand_over",
        )(*found)

    return jax.shard_map(
        local,
        mesh=mesh,
        in_specs=(
            P("clus", "probe", None),
            P("clus", None),
            P(None, "clus", None, None),
            P(None, "clus"),
            P("clus", None),
            P(None, None, "clus"),
            P(),
        ),
        out_specs=(P("clus", None), P(), P(None, "clus")),
        check_vma=False,
    )
```

```python
import functools

import jax
import jax.numpy as jnp
import numpy as np
from jax import lax
from jax.experimental import pallas as pl
from jax.experimental.pallas import tpu as pltpu
from jax.sharding import PartitionSpec as P

MESH = pl.DeviceIdType.MESH
CL = 12
SLOTS = 20
ROWS = 16
B = 128
CHIPS_Y = 4
ATOMS = 32
REACH = 12
ORDER = 4
PROBE_VECTORS = 128
DECAY = 50.0
SMEARING_TEMP = 0.1
QUAD_NODES = 64
EMPTY = CL * SLOTS
F32 = jnp.float32
BF16 = jnp.bfloat16
FAR, NEAR = 0, 1
LINK = BF16


def pair_offset(side, own, other):
    if side == FAR:
        return REACH - 1 - other - own if other + own <= REACH - 1 else None
    return 3 * REACH - 1 - other - own if other + own >= REACH - 1 else None


def kernel(
    clus, probe, probes_hbm, onsite_hbm, hop_ref, col_hbm, atom_hbm, bond_hbm, mu_hbm, cos_hbm,
    density_hbm, filling_hbm, forces_hbm,
    density_ref, filling_ref, forces_ref, mu_ref, probes_ref, onsite_ref, col_ref, atom_ref, bond_ref, cos_ref, atom_far, kbuf, ktbuf, tab_v, bond_v, tab, bond, xs, halo, part_out, part_in, cheb, fermi, y_acc, coef,
    norm_buf, norm_in, fill_buf, fill_in, dens_out, dens_in, force_acc, far_acc, ahead, col_out, col_in, onehot, z_out, z_in, f_out, f_in,
    isem, osem, ksem, tsem, asem, hs, hr, ps, pr, ns, nr, gs, gr, ds, dr, fs, fr, zs, zr, ws, wr, word,
):
    me = lax.axis_index("clus")
    z = lax.axis_index("probe")
    flip = me % 2
    sign = 1 - 2 * flip
    place = [flip * (CL - 1) + sign * c for c in range(CL)]
    chips = clus // 2
    chip = me // 2
    has_far = jnp.logical_and(me > 0, me < clus - 1)

    far_clus = (me + clus - sign) % clus
    far = (far_clus, z)
    near = (me + sign, z)
    chip_peers = [(((chip + q) % chips) * 2 + flip, z) for q in range(1, chips)]
    z_peers = [(me, (z + q) % probe) for q in range(1, probe)]
    far_peers = [(far_clus, (z + q) % probe) for q in range(probe)]

    chips_x = chips // CHIPS_Y
    cx, cy = chip // CHIPS_Y, chip % CHIPS_Y
    along_x = [((((cx + q) % chips_x) * CHIPS_Y + cy) * 2 + flip, z) for q in (1, chips_x - 1)]
    along_y = [((cx * CHIPS_Y + (cy + q) % CHIPS_Y) * 2 + flip, z) for q in (1, CHIPS_Y - 1)]
    along_z = [(me, (z + q) % probe) for q in (1, probe - 1)]
    rounds = [along_z + along_y, along_z + along_y, along_z + along_x, along_z + along_x]

    def spread(i):
        for peer in rounds[i]:
            pl.semaphore_signal(word.at[i], inc=1, device_id=peer, device_id_type=MESH)

    def heard(i):
        pl.semaphore_wait(word.at[i], len(rounds[i]))

    barrier = pltpu.get_barrier_semaphore()
    everyone = [near] + along_x + along_y + along_z
    for peer in everyone:
        pl.semaphore_signal(barrier, inc=1, device_id=peer, device_id_type=MESH)

    @pl.when(has_far)
    def _():
        pl.semaphore_signal(barrier, inc=1, device_id=far, device_id_type=MESH)

    def send(src, dst, s, r, peer):
        return pltpu.make_async_remote_copy(
            src_ref=src, dst_ref=dst, send_sem=s, recv_sem=r, device_id=peer, device_id_type=MESH
        )

    loads = [
        pltpu.make_async_copy(hop_ref.at[m], kbuf.at[pl.ds(m * CL, CL)], ksem.at[m]) for m in range(SLOTS)
    ]
    inputs = [
        pltpu.make_async_copy(source, target, isem.at[i])
        for i, (source, target) in enumerate(
            (
                (col_hbm, col_ref), (bond_hbm, bond_ref), (probes_hbm, probes_ref), (cos_hbm, cos_ref),
                (atom_hbm, atom_ref), (onsite_hbm, onsite_ref), (mu_hbm, mu_ref),
            )
        )
    ]
    for copy in inputs + loads:
        copy.start()
    for copy in inputs:
        copy.wait()

    lane = lax.broadcasted_iota(jnp.int32, (CL, SLOTS), 0)
    slot = lax.broadcasted_iota(jnp.int32, (CL, SLOTS), 1)
    columns = col_ref[...]
    rel = jnp.where(columns >= 0, columns - me * CL - lane + REACH, -1)
    rel = jnp.where(rel >= 0, rel * sign + flip * (2 * REACH), -1)
    flat = slot * CL + lane
    directions = [bond_ref[x].astype(F32) for x in range(3)]
    wide_lane = lax.broadcasted_iota(jnp.int32, (CL, B), 1)
    places = jnp.full((CL, B), EMPTY, jnp.int32)
    facing = [jnp.zeros((CL, B), F32)] * 3
    for o in range(2 * REACH + 1):
        hit = rel == o
        here = wide_lane == o
        places = jnp.where(here, jnp.min(jnp.where(hit, flat, EMPTY), axis=1, keepdims=True), places)
        for x in range(3):
            facing[x] = jnp.where(
                here, jnp.sum(jnp.where(hit, directions[x], 0.0), axis=1, keepdims=True), facing[x]
            )
    tab_v[0:CL, :] = places
    for x in range(3):
        bond_v[16 * x : 16 * x + CL, :] = facing[x]
    tables = [pltpu.make_async_copy(tab_v, tab, tsem.at[0]), pltpu.make_async_copy(bond_v, bond, tsem.at[1])]
    for copy in tables:
        copy.start()

    @pl.when(jnp.logical_not(has_far))
    def _():
        f_in[...] = jnp.zeros(f_in.shape, F32)
        atom_far[...] = jnp.zeros(atom_far.shape, jnp.int32)
        halo[:, FAR] = jnp.zeros((ORDER + 1, CL, ROWS, B), BF16)
        part_in[:, FAR] = jnp.zeros((ORDER, CL, ROWS, B), LINK)

    nacc = jnp.zeros((ROWS, B), F32)
    for c in range(CL):
        xc = probes_ref[place[c]]
        xs[0, c] = xc
        wide = xc.astype(F32)
        cheb[0, c] = wide
        cheb[1, c] = jnp.zeros((ROWS, B), F32)
        nacc = nacc + wide * wide
    norm_buf[0] = nacc

    occupation = 1.0 / (1.0 + jnp.exp((cos_ref[1:2, :] - mu_ref[0]) / SMEARING_TEMP))
    weight = lax.broadcasted_iota(jnp.int32, (8, B), 0)
    total = jnp.sum(cos_ref[...] * occupation, axis=1, keepdims=True) * (2.0 / QUAD_NODES)
    coef[...] = jnp.broadcast_to(total, (8, B)) * jnp.where(weight == 0, 0.5, 1.0)
    for c in range(CL):
        fermi[c] = cheb[0, c] * coef[0:1, :]

    pl.semaphore_wait(barrier, len(everyone) + has_far.astype(jnp.int32))

    def halo_copy(k, side):
        return send(xs.at[k], halo.at[k, side], hs.at[k, side], hr.at[k, side], (far, near)[side])

    def part_copy(k, side):
        return send(part_out.at[k, side], part_in.at[k, side], ps.at[k, side], pr.at[k, side], (far, near)[side])

    def stage_copies(own, arrived, s, r, stage, arriving=False):
        if stage == 0:
            return [send(own.at[0], arrived.at[chips], s.at[0], r.at[chips], near)]
        copies = []
        for q, peer in enumerate(chip_peers):
            place_in = (chip + chips - q - 1) % chips if arriving else chip
            copies.append(send(own.at[stage], arrived.at[place_in], s.at[1 + q], r.at[place_in], peer))
        return copies

    norm_copies = functools.partial(stage_copies, norm_buf, norm_in, ns, nr)

    def fill_copies(arriving=False):
        copies = []
        for q in range(1, clus):
            place_in = (me + clus - q) % clus if arriving else me
            copies.append(send(fill_buf, fill_in.at[place_in], gs.at[q], gr.at[place_in], ((me + q) % clus, z)))
        return copies


    def collect(copies, own, arrived, stage):
        for copy in copies(stage, True):
            copy.wait_recv()
        if stage == 0:
            own[1] = own[0] + arrived[chips]
            return
        arrived[chip] = own[stage]
        value = arrived[0]
        for q in range(1, chips):
            value = value + arrived[q]
        own[stage + 1] = value

    def atoms_copy():
        return send(atom_ref, atom_far, asem.at[0], asem.at[1], far)

    @pl.when(has_far)
    def _():
        halo_copy(0, FAR).start()
        atoms_copy().start()

    halo_copy(0, NEAR).start()
    for copy in norm_copies(0):
        copy.start()
    spread(0)

    kbuf[EMPTY] = jnp.zeros((B, B), BF16)
    ktbuf[EMPTY] = jnp.zeros((B, B), BF16)

    for copy in loads + tables:
        copy.wait()

    def straight(o, c):
        return kbuf[tab[place[c], o]]

    def turned(o, c):
        return ktbuf[tab[place[c], o]]

    def product(vectors, blocks):
        return jnp.dot(
            jnp.concatenate(vectors, axis=1), jnp.concatenate(blocks, axis=0), preferred_element_type=F32
        )

    def side_direct(k, side, c):
        others = [b for b in range(CL) if pair_offset(side, c, b) is not None]
        return product(
            [halo[k, side, b] for b in others], [turned(pair_offset(side, c, b), c) for b in others]
        )

    def partials(k):
        x = [xs[k, c] for c in range(CL)]
        for side in (FAR, NEAR):
            for b in range(CL):
                own = [c for c in range(CL) if pair_offset(side, c, b) is not None]
                part_out[k, side, b] = product(
                    [x[c] for c in own], [straight(pair_offset(side, c, b), c) for c in own]
                ).astype(LINK)
            if side == FAR:

                @pl.when(has_far)
                def _():
                    part_copy(k, FAR).start()

            else:
                part_copy(k, NEAR).start()

    partials(0)

    def turn(m, carry):
        for c in range(CL):
            ktbuf[m * CL + c] = kbuf[m * CL + c].T
        return carry

    lax.fori_loop(0, SLOTS, turn, 0)
    collect(norm_copies, norm_buf, norm_in, 0)

    def apply(k, carry):
        @pl.when(jnp.logical_and(k >= 1, has_far))
        def _():
            halo_copy(k, FAR).start()

        @pl.when(k >= 1)
        def _():
            halo_copy(k, NEAR).start()

        @pl.when(k >= 1)
        def _():
            partials(k)

        x = [xs[k, c] for c in range(CL)]
        for c in range(CL):
            y_acc[c] = product(
                x + x,
                [turned(REACH + d - c, c) for d in range(CL)] + [straight(REACH + c - d, d) for d in range(CL)],
            )

        @pl.when(k == 0)
        def _():
            heard(0)
            spread(1)

        @pl.when(k == 1)
        def _():
            heard(1)
            spread(2)

        @pl.when(k == 2)
        def _():
            heard(2)
            spread(3)
            for copy in norm_copies(1):
                copy.start()

        @pl.when(k == 3)
        def _():
            heard(3)

        halo_copy(k, NEAR).wait_recv()
        for c in range(CL):
            y_acc[c] = y_acc[c] + side_direct(k, NEAR, c)
        part_copy(k, NEAR).wait_recv()

        @pl.when(has_far)
        def _():
            halo_copy(k, FAR).wait_recv()

        for c in range(CL):
            y_acc[c] = y_acc[c] + part_in[k, NEAR, c].astype(F32) + side_direct(k, FAR, c)

        @pl.when(has_far)
        def _():
            part_copy(k, FAR).wait_recv()

        alpha = jnp.where(k == 0, 1.0, 2.0)
        into = (k + 1) % 2
        for c in range(CL):
            image = y_acc[c] + part_in[k, FAR, c].astype(F32)
            image = image + onsite_ref[pl.ds(place[c], 1), :] * xs[k, c].astype(F32)
            following = alpha * image - cheb[into, c]
            cheb[into, c] = following
            fermi[c] = fermi[c] + coef[pl.ds(k + 1, 1), :] * following
            xs[k + 1, c] = following.astype(BF16)
        return carry

    lax.fori_loop(0, ORDER, apply, 0)

    collect(norm_copies, norm_buf, norm_in, 1)
    norm_sq = jnp.sum(norm_buf[2], axis=1, keepdims=True)
    scale = jnp.broadcast_to((clus * CL * B) / (norm_sq * PROBE_VECTORS), (ROWS, B))
    for c in range(CL):
        scaled = fermi[c] * scale
        fermi[c] = scaled
        xs[ORDER, c] = scaled.astype(BF16)

    @pl.when(has_far)
    def _():
        halo_copy(ORDER, FAR).start()

    halo_copy(ORDER, NEAR).start()
    dens_out[...] = jnp.zeros(dens_out.shape, F32)
    for c in range(CL):
        row = jnp.sum(xs[0, c].astype(F32) * fermi[c], axis=0, keepdims=True)
        dens_out[c : c + 1, :] = row

    def z_copies(src, dst, s, r, arriving=False):
        copies = []
        for q, peer in enumerate(z_peers):
            slot = (z + probe - q - 1) % probe if arriving else z
            copies.append(send(src, dst.at[slot], s.at[q], r.at[slot], peer))
        return copies

    def z_sum(src, dst, s, r):
        dst[z] = src[...]
        for copy in z_copies(src, dst, s, r, True):
            copy.wait_recv()
        value = dst[0]
        for q in range(1, probe):
            value = value + dst[q]
        return value

    for copy in z_copies(dens_out, dens_in, ds, dr):
        copy.start()

    far_pairs = [(c, b) for b in range(CL) for c in range(CL) if pair_offset(FAR, c, b) is not None]

    def sums(left, block, u, v):
        image = jnp.dot(left, block, preferred_element_type=F32)
        r = v * image[:ROWS] + u * image[ROWS:]
        return r[:8] + r[8:]

    both = [jnp.concatenate([xs[0, c], xs[ORDER, c]], axis=0) for c in range(CL)]

    def own_vectors(c):
        return xs[0, c].astype(F32), xs[ORDER, c].astype(F32)

    def add(acc, o, c, r, positive):
        out = []
        for x in range(3):
            term = bond[16 * x + place[c], o] * r
            out.append(acc[x] + term if positive else acc[x] - term)
        return out

    zero3 = [jnp.zeros((8, B), F32)] * 3
    for c in range(CL):
        u, v = own_vectors(c)
        acc = zero3
        for d in range(CL):
            o = REACH + d - c
            acc = add(acc, o, c, sums(both[d], turned(o, c), u, v), False)
        for d in range(CL):
            o = REACH + c - d
            acc = add(acc, o, d, sums(both[d], straight(o, d), u, v), True)
        for x in range(3):
            force_acc[c, x] = acc[x]

    def col_copy():
        return send(col_out, col_in, fs.at[0], fr.at[0], near)

    row = lax.broadcasted_iota(jnp.int32, (B, B), 0)

    @pl.when(has_far)
    def _():
        atoms_copy().wait_recv()

    for c in range(CL):
        onehot[0, c] = (row == atom_ref[c : c + 1, :] + ATOMS * (c % 4)).astype(BF16)
        onehot[1, c] = (row == atom_far[c : c + 1, :] + ATOMS * (c % 4)).astype(BF16)

    dims = (((1,), (1,)), ((), ()))
    pick = lax.broadcasted_iota(jnp.int32, (8, B), 0)

    def atom_sums(which, source, target):
        for quad in range(CL // 4):
            pieces = []
            for c in range(quad * 4, quad * 4 + 4):
                value = jnp.where(pick == 0, source(c, 0), jnp.where(pick == 1, source(c, 1), source(c, 2)))
                high = value.astype(BF16).astype(F32)
                rest = value - high
                middle = rest.astype(BF16).astype(F32)
                pieces.append(jnp.concatenate([high, middle, rest - middle, jnp.zeros((8, B), F32)], axis=0).astype(BF16))
            owners = jnp.concatenate([onehot[which, c] for c in range(quad * 4, quad * 4 + 4)], axis=1)
            total = lax.dot_general(jnp.concatenate(pieces, axis=1), owners, dims, preferred_element_type=F32)
            total = total[0:8] + total[8:16] + total[16:24]
            target[quad * 3 : quad * 3 + 3, :] = total[0:3]

    def far_copies(arriving=False):
        copies = []
        for q, peer in enumerate(far_peers):
            place_in = (z + probe - q) % probe if arriving else z
            copies.append(send(f_out, f_in.at[place_in], ws.at[q], wr.at[place_in], peer))
        return copies

    def halo_both(side, b):
        return jnp.concatenate([halo[0, side, b], halo[ORDER, side, b]], axis=0)

    z_out[...] = jnp.zeros(z_out.shape, F32)
    f_out[...] = jnp.zeros(f_out.shape, F32)
    for side in (NEAR, FAR):
        if side == NEAR:
            halo_copy(ORDER, NEAR).wait_recv()
        else:
            for i, (c, b) in enumerate(far_pairs):
                ahead[i] = jnp.dot(both[c], straight(pair_offset(FAR, c, b), c), preferred_element_type=F32)

            @pl.when(has_far)
            def _():
                halo_copy(ORDER, FAR).wait_recv()

        for b in range(CL):
            u, v = halo[0, side, b].astype(F32), halo[ORDER, side, b].astype(F32)
            acc = zero3
            for c in range(CL):
                o = pair_offset(side, c, b)
                if o is not None and side == NEAR:
                    acc = add(acc, o, c, sums(both[c], straight(o, c), u, v), True)
                elif o is not None:
                    image = ahead[far_pairs.index((c, b))]
                    r = v * image[:ROWS] + u * image[ROWS:]
                    acc = add(acc, o, c, r[:8] + r[8:], True)
            for x in range(3):
                total = jnp.sum(acc[x], axis=0, keepdims=True)
                if side == NEAR:
                    col_out[3 * b + x : 3 * b + x + 1, :] = total
                else:
                    far_acc[b, x] = jnp.broadcast_to(total * DECAY, (8, B))
        if side == NEAR:
            col_copy().start()
        else:
            atom_sums(1, lambda c, x: far_acc[(1 - flip) * (CL - 1) - sign * c, x], f_out)

            @pl.when(has_far)
            def _():
                for copy in far_copies():
                    copy.start()

        for c in range(CL):
            u, v = own_vectors(c)
            acc = [force_acc[c, x] for x in range(3)]
            for b in range(CL):
                o = pair_offset(side, c, b)
                if o is not None:
                    acc = add(acc, o, c, sums(halo_both(side, b), turned(o, c), u, v), False)
            for x in range(3):
                force_acc[c, x] = acc[x]

    col_copy().wait_recv()
    for c in range(CL):
        for x in range(3):
            j = 3 * c + x
            value = jnp.sum(force_acc[c, x], axis=0, keepdims=True) + col_in[j : j + 1, :]
            force_acc[c, x] = jnp.broadcast_to(value * DECAY, (8, B))
    atom_sums(0, lambda c, x: force_acc[place[c], x], z_out)
    for copy in z_copies(z_out, z_in, zs, zr):
        copy.start()

    summed = z_sum(dens_out, dens_in, ds, dr)
    for c in range(CL):
        density_ref[pl.ds(place[c], 1), :] = summed[c : c + 1, :]
    results = [
        pltpu.make_async_copy(source, target, osem.at[i])
        for i, (source, target) in enumerate(
            ((density_ref, density_hbm), (forces_ref, forces_hbm), (filling_ref, filling_hbm))
        )
    ]
    results[0].start()
    fill_buf[...] = summed[0:8] + summed[8:16]
    for copy in fill_copies():
        copy.start()
    fill_in[me] = fill_buf[...]

    @pl.when(has_far)
    def _():
        for copy in far_copies(True):
            copy.wait_recv()

    summed = z_sum(z_out, z_in, zs, zr)
    for q in range(probe):
        summed = summed + f_in[q]
    for quad in range(CL // 4):
        forces_ref[:, quad * B : (quad + 1) * B] = summed[quad * 3 : quad * 3 + 3]
    results[1].start()
    for copy in fill_copies(True):
        copy.wait_recv()
    filled = fill_in[0]
    for q in range(1, clus):
        filled = filled + fill_in[q]
    filling_ref[0] = jnp.sum(filled) / (clus * CL * B)
    results[2].start()

    def finish(k, carry):
        halo_copy(k, NEAR).wait_send()
        part_copy(k, NEAR).wait_send()

        @pl.when(has_far)
        def _():
            halo_copy(k, FAR).wait_send()
            part_copy(k, FAR).wait_send()

        return carry

    lax.fori_loop(0, ORDER, finish, 0)
    halo_copy(ORDER, NEAR).wait_send()
    col_copy().wait_send()

    @pl.when(has_far)
    def _():
        halo_copy(ORDER, FAR).wait_send()
        atoms_copy().wait_send()
        for copy in far_copies():
            copy.wait_send()

    for stage in range(2):
        for copy in norm_copies(stage):
            copy.wait_send()
    for copy in fill_copies():
        copy.wait_send()
    for copy in z_copies(dens_out, dens_in, ds, dr) + z_copies(z_out, z_in, zs, zr):
        copy.wait_send()
    for copy in results:
        copy.wait()


def hand_over(density, filling, forces, density_out, filling_out, forces_out, sems):
    copies = [
        pltpu.make_async_copy(source, target, sems.at[i])
        for i, (source, target) in enumerate(((density, density_out), (filling, filling_out), (forces, forces_out)))
    ]
    for copy in copies:
        copy.start()
    for copy in copies:
        copy.wait()


def cosines():
    angles = np.pi * (np.arange(QUAD_NODES) + 0.5) / QUAD_NODES
    table = np.zeros((8, B), np.float32)
    for k in range(ORDER + 1):
        table[k, :QUAD_NODES] = np.cos(k * angles)
    return table


def solution(mesh):
    clus, probe = mesh.shape["clus"], mesh.shape["probe"]
    small = 1 + clus // 2
    vmem, dma = pltpu.VMEM, pltpu.SemaphoreType.DMA

    def local(probes, onsite, hopping, block_col, atom_of, bond_dir, chemical_potential):
        in_hbm = pl.BlockSpec(memory_space=pltpu.HBM)
        shapes = (
            jax.ShapeDtypeStruct((CL, B), F32),
            jax.ShapeDtypeStruct((1,), F32),
            jax.ShapeDtypeStruct((3, CL * ATOMS), F32),
        )
        found = pl.pallas_call(
            functools.partial(kernel, clus, probe),
            out_shape=shapes,
            in_specs=[in_hbm] * 8,
            out_specs=(in_hbm,) * 3,
            scratch_shapes=[
                vmem((CL, B), F32),
                pltpu.SMEM((1,), F32),
                vmem((3, CL * ATOMS), F32),
                pltpu.SMEM((1,), F32),
                vmem((CL, ROWS, B), BF16),
                vmem((CL, B), F32),
                vmem((CL, SLOTS), jnp.int32),
                vmem((CL, B), jnp.int32),
                vmem((3, CL, SLOTS), BF16),
                vmem((8, B), F32),
                vmem((CL, B), jnp.int32),
                vmem((EMPTY + 1, B, B), BF16),
                vmem((EMPTY + 1, B, B), BF16),
                vmem((16, B), jnp.int32),
                vmem((48, B), F32),
                pltpu.SMEM((16, B), jnp.int32),
                pltpu.SMEM((48, B), F32),
                vmem((ORDER + 1, CL, ROWS, B), BF16),
                vmem((ORDER + 1, 2, CL, ROWS, B), BF16),
                vmem((ORDER, 2, CL, ROWS, B), LINK),
                vmem((ORDER, 2, CL, ROWS, B), LINK),
                vmem((2, CL, ROWS, B), F32),
                vmem((CL, ROWS, B), F32),
                vmem((CL, ROWS, B), F32),
                vmem((8, B), F32),
                vmem((3, ROWS, B), F32),
                vmem((small, ROWS, B), F32),
                vmem((8, B), F32),
                vmem((clus, 8, B), F32),
                vmem((16, B), F32),
                vmem((probe, 16, B), F32),
                vmem((CL, 3, 8, B), F32),
                vmem((CL, 3, 8, B), F32),
                vmem((CL * (CL + 1) // 2, 2 * ROWS, B), F32),
                vmem((40, B), F32),
                vmem((40, B), F32),
                vmem((2, CL, B, B), BF16),
                vmem((16, B), F32),
                vmem((probe, 16, B), F32),
                vmem((16, B), F32),
                vmem((probe, 16, B), F32),
                dma((7,)),
                dma((3,)),
                dma((SLOTS,)),
                dma((2,)),
                dma((2,)),
                dma((ORDER + 1, 2)),
                dma((ORDER + 1, 2)),
                dma((ORDER, 2)),
                dma((ORDER, 2)),
                dma((small,)),
                dma((small,)),
                dma((clus,)),
                dma((clus,)),
                dma((probe,)),
                dma((probe,)),
                dma((1,)),
                dma((1,)),
                dma((probe,)),
                dma((probe,)),
                dma((probe,)),
                dma((probe,)),
                pltpu.SemaphoreType.REGULAR((4,)),
            ],
            compiler_params=pltpu.CompilerParams(
                collective_id=0, has_side_effects=True, vmem_limit_bytes=60 * 1024 * 1024
            ),
            cost_estimate=pl.CostEstimate(flops=2_600_000_000, bytes_accessed=8_500_000, transcendentals=0),
            name="fermi_forces",
        )(
            probes, onsite, hopping, block_col.T, atom_of, jnp.swapaxes(bond_dir, 1, 2), chemical_potential,
            jnp.asarray(cosines()),
        )
        return pl.pallas_call(
            hand_over,
            out_shape=shapes,
            in_specs=[in_hbm] * 3,
            out_specs=(in_hbm,) * 3,
            scratch_shapes=[dma((3,))],
            compiler_params=pltpu.CompilerParams(vmem_limit_bytes=60 * 1024 * 1024),
            name="hand_over",
        )(*found)

    return jax.shard_map(
        local,
        mesh=mesh,
        in_specs=(
            P("clus", "probe", None),
            P("clus", None),
            P(None, "clus", None, None),
            P(None, "clus"),
            P("clus", None),
            P(None, None, "clus"),
            P(),
        ),
        out_specs=(P("clus", None), P(), P(None, "clus")),
        check_vma=False,
    )
```

```python
import functools

import jax
import jax.numpy as jnp
import numpy as np
from jax import lax
from jax.experimental import pallas as pl
from jax.experimental.pallas import tpu as pltpu
from jax.sharding import PartitionSpec as P

MESH = pl.DeviceIdType.MESH
CL = 12
SLOTS = 20
ROWS = 16
B = 128
CHIPS_Y = 4
ATOMS = 32
REACH = 12
ORDER = 4
PROBE_VECTORS = 128
DECAY = 50.0
SMEARING_TEMP = 0.1
QUAD_NODES = 64
EMPTY = CL * SLOTS
F32 = jnp.float32
BF16 = jnp.bfloat16
FAR, NEAR = 0, 1
LINK = BF16


def pair_offset(side, own, other):
    if side == FAR:
        return REACH - 1 - other - own if other + own <= REACH - 1 else None
    return 3 * REACH - 1 - other - own if other + own >= REACH - 1 else None


def kernel(
    clus, probe, probes_hbm, onsite_hbm, hop_ref, col_hbm, atom_hbm, bond_hbm, mu_hbm, cos_hbm,
    density_hbm, z_in, f_in, fill_in,
    density_ref, mu_ref, probes_ref, onsite_ref, col_ref, atom_ref, bond_ref, cos_ref, atom_far, kbuf, ktbuf, tab_v, bond_v, tab, bond, xs, halo, part_out, part_in, cheb, fermi, y_acc, coef,
    norm_buf, norm_in, fill_buf, dens_out, dens_in, force_acc, far_acc, ahead, col_out, col_in, onehot, z_out, f_out,
    isem, osem, ksem, tsem, asem, hs, hr, ps, pr, ns, nr, gs, gr, ds, dr, fs, fr, zs, zr, ws, wr, word,
):
    me = lax.axis_index("clus")
    z = lax.axis_index("probe")
    flip = me % 2
    sign = 1 - 2 * flip
    place = [flip * (CL - 1) + sign * c for c in range(CL)]
    chips = clus // 2
    chip = me // 2
    has_far = jnp.logical_and(me > 0, me < clus - 1)

    far_clus = (me + clus - sign) % clus
    far = (far_clus, z)
    near = (me + sign, z)
    chip_peers = [(((chip + q) % chips) * 2 + flip, z) for q in range(1, chips)]
    z_peers = [(me, (z + q) % probe) for q in range(1, probe)]
    far_peers = [(far_clus, (z + q) % probe) for q in range(probe)]

    chips_x = chips // CHIPS_Y
    cx, cy = chip // CHIPS_Y, chip % CHIPS_Y
    along_x = [((((cx + q) % chips_x) * CHIPS_Y + cy) * 2 + flip, z) for q in (1, chips_x - 1)]
    along_y = [((cx * CHIPS_Y + (cy + q) % CHIPS_Y) * 2 + flip, z) for q in (1, CHIPS_Y - 1)]
    along_z = [(me, (z + q) % probe) for q in (1, probe - 1)]
    rounds = [along_z + along_y, along_z + along_y, along_z + along_x, along_z + along_x]

    def spread(i):
        for peer in rounds[i]:
            pl.semaphore_signal(word.at[i], inc=1, device_id=peer, device_id_type=MESH)

    def heard(i):
        pl.semaphore_wait(word.at[i], len(rounds[i]))

    barrier = pltpu.get_barrier_semaphore()
    everyone = [near] + along_x + along_y + along_z
    for peer in everyone:
        pl.semaphore_signal(barrier, inc=1, device_id=peer, device_id_type=MESH)

    @pl.when(has_far)
    def _():
        pl.semaphore_signal(barrier, inc=1, device_id=far, device_id_type=MESH)

    def send(src, dst, s, r, peer):
        return pltpu.make_async_remote_copy(
            src_ref=src, dst_ref=dst, send_sem=s, recv_sem=r, device_id=peer, device_id_type=MESH
        )

    loads = [
        pltpu.make_async_copy(hop_ref.at[m], kbuf.at[pl.ds(m * CL, CL)], ksem.at[m]) for m in range(SLOTS)
    ]
    inputs = [
        pltpu.make_async_copy(source, target, isem.at[i])
        for i, (source, target) in enumerate(
            (
                (col_hbm, col_ref), (bond_hbm, bond_ref), (probes_hbm, probes_ref), (cos_hbm, cos_ref),
                (atom_hbm, atom_ref), (onsite_hbm, onsite_ref), (mu_hbm, mu_ref),
            )
        )
    ]
    for copy in inputs + loads:
        copy.start()
    for copy in inputs:
        copy.wait()

    lane = lax.broadcasted_iota(jnp.int32, (CL, SLOTS), 0)
    slot = lax.broadcasted_iota(jnp.int32, (CL, SLOTS), 1)
    columns = col_ref[...]
    rel = jnp.where(columns >= 0, columns - me * CL - lane + REACH, -1)
    rel = jnp.where(rel >= 0, rel * sign + flip * (2 * REACH), -1)
    flat = slot * CL + lane
    directions = [bond_ref[x].astype(F32) for x in range(3)]
    wide_lane = lax.broadcasted_iota(jnp.int32, (CL, B), 1)
    places = jnp.full((CL, B), EMPTY, jnp.int32)
    facing = [jnp.zeros((CL, B), F32)] * 3
    for o in range(2 * REACH + 1):
        hit = rel == o
        here = wide_lane == o
        places = jnp.where(here, jnp.min(jnp.where(hit, flat, EMPTY), axis=1, keepdims=True), places)
        for x in range(3):
            facing[x] = jnp.where(
                here, jnp.sum(jnp.where(hit, directions[x], 0.0), axis=1, keepdims=True), facing[x]
            )
    tab_v[0:CL, :] = places
    for x in range(3):
        bond_v[16 * x : 16 * x + CL, :] = facing[x]
    tables = [pltpu.make_async_copy(tab_v, tab, tsem.at[0]), pltpu.make_async_copy(bond_v, bond, tsem.at[1])]
    for copy in tables:
        copy.start()

    @pl.when(jnp.logical_not(has_far))
    def _():
        atom_far[...] = jnp.zeros(atom_far.shape, jnp.int32)
        halo[:, FAR] = jnp.zeros((ORDER + 1, CL, ROWS, B), BF16)
        part_in[:, FAR] = jnp.zeros((ORDER, CL, ROWS, B), LINK)

    nacc = jnp.zeros((ROWS, B), F32)
    for c in range(CL):
        xc = probes_ref[place[c]]
        xs[0, c] = xc
        wide = xc.astype(F32)
        cheb[0, c] = wide
        cheb[1, c] = jnp.zeros((ROWS, B), F32)
        nacc = nacc + wide * wide
    norm_buf[0] = nacc

    occupation = 1.0 / (1.0 + jnp.exp((cos_ref[1:2, :] - mu_ref[0]) / SMEARING_TEMP))
    weight = lax.broadcasted_iota(jnp.int32, (8, B), 0)
    total = jnp.sum(cos_ref[...] * occupation, axis=1, keepdims=True) * (2.0 / QUAD_NODES)
    coef[...] = jnp.broadcast_to(total, (8, B)) * jnp.where(weight == 0, 0.5, 1.0)
    for c in range(CL):
        fermi[c] = cheb[0, c] * coef[0:1, :]

    pl.semaphore_wait(barrier, len(everyone) + has_far.astype(jnp.int32))

    def halo_copy(k, side):
        return send(xs.at[k], halo.at[k, side], hs.at[k, side], hr.at[k, side], (far, near)[side])

    def part_copy(k, side):
        return send(part_out.at[k, side], part_in.at[k, side], ps.at[k, side], pr.at[k, side], (far, near)[side])

    def stage_copies(own, arrived, s, r, stage, arriving=False):
        if stage == 0:
            return [send(own.at[0], arrived.at[chips], s.at[0], r.at[chips], near)]
        copies = []
        for q, peer in enumerate(chip_peers):
            place_in = (chip + chips - q - 1) % chips if arriving else chip
            copies.append(send(own.at[stage], arrived.at[place_in], s.at[1 + q], r.at[place_in], peer))
        return copies

    norm_copies = functools.partial(stage_copies, norm_buf, norm_in, ns, nr)

    def fill_copies(arriving=False):
        copies = []
        for q in range(1, clus):
            place_in = (me + clus - q) % clus if arriving else me
            copies.append(send(fill_buf, fill_in.at[place_in], gs.at[q], gr.at[place_in], ((me + q) % clus, z)))
        return copies


    def collect(copies, own, arrived, stage):
        for copy in copies(stage, True):
            copy.wait_recv()
        if stage == 0:
            own[1] = own[0] + arrived[chips]
            return
        arrived[chip] = own[stage]
        value = arrived[0]
        for q in range(1, chips):
            value = value + arrived[q]
        own[stage + 1] = value

    def atoms_copy():
        return send(atom_ref, atom_far, asem.at[0], asem.at[1], far)

    @pl.when(has_far)
    def _():
        halo_copy(0, FAR).start()
        atoms_copy().start()

    halo_copy(0, NEAR).start()
    for copy in norm_copies(0):
        copy.start()
    spread(0)

    kbuf[EMPTY] = jnp.zeros((B, B), BF16)
    ktbuf[EMPTY] = jnp.zeros((B, B), BF16)

    for copy in loads + tables:
        copy.wait()

    def straight(o, c):
        return kbuf[tab[place[c], o]]

    def turned(o, c):
        return ktbuf[tab[place[c], o]]

    def product(vectors, blocks):
        return jnp.dot(
            jnp.concatenate(vectors, axis=1), jnp.concatenate(blocks, axis=0), preferred_element_type=F32
        )

    def side_direct(k, side, c):
        others = [b for b in range(CL) if pair_offset(side, c, b) is not None]
        return product(
            [halo[k, side, b] for b in others], [turned(pair_offset(side, c, b), c) for b in others]
        )

    def partials(k):
        x = [xs[k, c] for c in range(CL)]
        for side in (FAR, NEAR):
            for b in range(CL):
                own = [c for c in range(CL) if pair_offset(side, c, b) is not None]
                part_out[k, side, b] = product(
                    [x[c] for c in own], [straight(pair_offset(side, c, b), c) for c in own]
                ).astype(LINK)
            if side == FAR:

                @pl.when(has_far)
                def _():
                    part_copy(k, FAR).start()

            else:
                part_copy(k, NEAR).start()

    partials(0)

    def turn(m, carry):
        for i in range(5):
            for c in range(CL):
                ktbuf[(5 * m + i) * CL + c] = kbuf[(5 * m + i) * CL + c].T
        return carry

    lax.fori_loop(0, SLOTS // 5, turn, 0)
    collect(norm_copies, norm_buf, norm_in, 0)

    def apply(k, carry):
        @pl.when(jnp.logical_and(k >= 1, has_far))
        def _():
            halo_copy(k, FAR).start()

        @pl.when(k >= 1)
        def _():
            halo_copy(k, NEAR).start()

        @pl.when(k >= 1)
        def _():
            partials(k)

        x = [xs[k, c] for c in range(CL)]
        for c in range(CL):
            y_acc[c] = product(
                x + x,
                [turned(REACH + d - c, c) for d in range(CL)] + [straight(REACH + c - d, d) for d in range(CL)],
            )

        @pl.when(k == 0)
        def _():
            heard(0)
            spread(1)

        @pl.when(k == 1)
        def _():
            heard(1)
            spread(2)

        @pl.when(k == 2)
        def _():
            heard(2)
            spread(3)
            for copy in norm_copies(1):
                copy.start()

        @pl.when(k == 3)
        def _():
            heard(3)

        halo_copy(k, NEAR).wait_recv()
        for c in range(CL):
            y_acc[c] = y_acc[c] + side_direct(k, NEAR, c)
        part_copy(k, NEAR).wait_recv()

        @pl.when(has_far)
        def _():
            halo_copy(k, FAR).wait_recv()

        for c in range(CL):
            y_acc[c] = y_acc[c] + part_in[k, NEAR, c].astype(F32) + side_direct(k, FAR, c)

        @pl.when(has_far)
        def _():
            part_copy(k, FAR).wait_recv()

        alpha = jnp.where(k == 0, 1.0, 2.0)
        into = (k + 1) % 2
        for c in range(CL):
            image = y_acc[c] + part_in[k, FAR, c].astype(F32)
            image = image + onsite_ref[pl.ds(place[c], 1), :] * xs[k, c].astype(F32)
            following = alpha * image - cheb[into, c]
            cheb[into, c] = following
            fermi[c] = fermi[c] + coef[pl.ds(k + 1, 1), :] * following
            xs[k + 1, c] = following.astype(BF16)
        return carry

    lax.fori_loop(0, ORDER, apply, 0)

    collect(norm_copies, norm_buf, norm_in, 1)
    norm_sq = jnp.sum(norm_buf[2], axis=1, keepdims=True)
    scale = jnp.broadcast_to((clus * CL * B) / (norm_sq * PROBE_VECTORS), (ROWS, B))
    for c in range(CL):
        scaled = fermi[c] * scale
        fermi[c] = scaled
        xs[ORDER, c] = scaled.astype(BF16)

    @pl.when(has_far)
    def _():
        halo_copy(ORDER, FAR).start()

    halo_copy(ORDER, NEAR).start()
    dens_out[...] = jnp.zeros(dens_out.shape, F32)
    for c in range(CL):
        row = jnp.sum(xs[0, c].astype(F32) * fermi[c], axis=0, keepdims=True)
        dens_out[c : c + 1, :] = row

    def z_copies(src, dst, s, r, arriving=False):
        copies = []
        for q, peer in enumerate(z_peers):
            slot = (z + probe - q - 1) % probe if arriving else z
            copies.append(send(src, dst.at[slot], s.at[q], r.at[slot], peer))
        return copies

    def z_sum(src, dst, s, r):
        dst[z] = src[...]
        for copy in z_copies(src, dst, s, r, True):
            copy.wait_recv()
        value = dst[0]
        for q in range(1, probe):
            value = value + dst[q]
        return value

    for copy in z_copies(dens_out, dens_in, ds, dr):
        copy.start()

    far_pairs = [(c, b) for b in range(CL) for c in range(CL) if pair_offset(FAR, c, b) is not None]

    def sums(left, block, u, v):
        image = jnp.dot(left, block, preferred_element_type=F32)
        r = v * image[:ROWS] + u * image[ROWS:]
        return r[:8] + r[8:]

    both = [jnp.concatenate([xs[0, c], xs[ORDER, c]], axis=0) for c in range(CL)]

    def own_vectors(c):
        return xs[0, c].astype(F32), xs[ORDER, c].astype(F32)

    def add(acc, o, c, r, positive):
        out = []
        for x in range(3):
            term = bond[16 * x + place[c], o] * r
            out.append(acc[x] + term if positive else acc[x] - term)
        return out

    zero3 = [jnp.zeros((8, B), F32)] * 3
    for c in range(CL):
        u, v = own_vectors(c)
        acc = zero3
        for d in range(CL):
            o = REACH + d - c
            acc = add(acc, o, c, sums(both[d], turned(o, c), u, v), False)
        for d in range(CL):
            o = REACH + c - d
            acc = add(acc, o, d, sums(both[d], straight(o, d), u, v), True)
        for x in range(3):
            force_acc[c, x] = acc[x]

    def col_copy():
        return send(col_out, col_in, fs.at[0], fr.at[0], near)

    row = lax.broadcasted_iota(jnp.int32, (B, B), 0)

    @pl.when(has_far)
    def _():
        atoms_copy().wait_recv()

    for c in range(CL):
        onehot[0, c] = (row == atom_ref[c : c + 1, :] + ATOMS * (c % 4)).astype(BF16)
        onehot[1, c] = (row == atom_far[c : c + 1, :] + ATOMS * (c % 4)).astype(BF16)

    dims = (((1,), (1,)), ((), ()))
    pick = lax.broadcasted_iota(jnp.int32, (8, B), 0)

    def atom_sums(which, source, target):
        for quad in range(CL // 4):
            pieces = []
            for c in range(quad * 4, quad * 4 + 4):
                value = jnp.where(pick == 0, source(c, 0), jnp.where(pick == 1, source(c, 1), source(c, 2)))
                high = value.astype(BF16).astype(F32)
                rest = value - high
                middle = rest.astype(BF16).astype(F32)
                pieces.append(jnp.concatenate([high, middle, rest - middle, jnp.zeros((8, B), F32)], axis=0).astype(BF16))
            owners = jnp.concatenate([onehot[which, c] for c in range(quad * 4, quad * 4 + 4)], axis=1)
            total = lax.dot_general(jnp.concatenate(pieces, axis=1), owners, dims, preferred_element_type=F32)
            total = total[0:8] + total[8:16] + total[16:24]
            target[quad * 3 : quad * 3 + 3, :] = total[0:3]

    def far_copies(arriving=False):
        copies = []
        for q, peer in enumerate(far_peers):
            place_in = (z + probe - q) % probe if arriving else z
            copies.append(send(f_out, f_in.at[place_in], ws.at[q], wr.at[place_in], peer))
        return copies

    def halo_both(side, b):
        return jnp.concatenate([halo[0, side, b], halo[ORDER, side, b]], axis=0)

    z_out[...] = jnp.zeros(z_out.shape, F32)
    f_out[...] = jnp.zeros(f_out.shape, F32)
    for side in (NEAR, FAR):
        if side == NEAR:
            halo_copy(ORDER, NEAR).wait_recv()
        else:
            for i, (c, b) in enumerate(far_pairs):
                ahead[i] = jnp.dot(both[c], straight(pair_offset(FAR, c, b), c), preferred_element_type=F32)

            @pl.when(has_far)
            def _():
                halo_copy(ORDER, FAR).wait_recv()

        for b in range(CL):
            u, v = halo[0, side, b].astype(F32), halo[ORDER, side, b].astype(F32)
            acc = zero3
            for c in range(CL):
                o = pair_offset(side, c, b)
                if o is not None and side == NEAR:
                    acc = add(acc, o, c, sums(both[c], straight(o, c), u, v), True)
                elif o is not None:
                    image = ahead[far_pairs.index((c, b))]
                    r = v * image[:ROWS] + u * image[ROWS:]
                    acc = add(acc, o, c, r[:8] + r[8:], True)
            for x in range(3):
                total = jnp.sum(acc[x], axis=0, keepdims=True)
                if side == NEAR:
                    col_out[3 * b + x : 3 * b + x + 1, :] = total
                else:
                    far_acc[b, x] = jnp.broadcast_to(total * DECAY, (8, B))
        if side == NEAR:
            col_copy().start()
        else:
            atom_sums(1, lambda c, x: far_acc[(1 - flip) * (CL - 1) - sign * c, x], f_out)

            @pl.when(has_far)
            def _():
                for copy in far_copies():
                    copy.start()

        for c in range(CL):
            u, v = own_vectors(c)
            acc = [force_acc[c, x] for x in range(3)]
            for b in range(CL):
                o = pair_offset(side, c, b)
                if o is not None:
                    acc = add(acc, o, c, sums(halo_both(side, b), turned(o, c), u, v), False)
            for x in range(3):
                force_acc[c, x] = acc[x]

    col_copy().wait_recv()
    for c in range(CL):
        for x in range(3):
            j = 3 * c + x
            value = jnp.sum(force_acc[c, x], axis=0, keepdims=True) + col_in[j : j + 1, :]
            force_acc[c, x] = jnp.broadcast_to(value * DECAY, (8, B))
    atom_sums(0, lambda c, x: force_acc[place[c], x], z_out)
    for copy in z_copies(z_out, z_in, zs, zr):
        copy.start()

    summed = z_sum(dens_out, dens_in, ds, dr)
    for c in range(CL):
        density_ref[pl.ds(place[c], 1), :] = summed[c : c + 1, :]
    fill_buf[...] = summed[0:8] + summed[8:16]
    for copy in fill_copies():
        copy.start()
    results = [
        pltpu.make_async_copy(source, target, osem.at[i])
        for i, (source, target) in enumerate(
            ((density_ref, density_hbm), (fill_buf, fill_in.at[me]), (z_out, z_in.at[z]))
        )
    ]
    for copy in results:
        copy.start()

    @pl.when(has_far)
    def _():
        for copy in far_copies(True):
            copy.wait_recv()

    for copy in z_copies(z_out, z_in, zs, zr, True) + fill_copies(True):
        copy.wait_recv()

    def finish(k, carry):
        halo_copy(k, NEAR).wait_send()
        part_copy(k, NEAR).wait_send()

        @pl.when(has_far)
        def _():
            halo_copy(k, FAR).wait_send()
            part_copy(k, FAR).wait_send()

        return carry

    lax.fori_loop(0, ORDER, finish, 0)
    halo_copy(ORDER, NEAR).wait_send()
    col_copy().wait_send()

    @pl.when(has_far)
    def _():
        halo_copy(ORDER, FAR).wait_send()
        atoms_copy().wait_send()
        for copy in far_copies():
            copy.wait_send()

    for stage in range(2):
        for copy in norm_copies(stage):
            copy.wait_send()
    for copy in fill_copies():
        copy.wait_send()
    for copy in z_copies(dens_out, dens_in, ds, dr) + z_copies(z_out, z_in, zs, zr):
        copy.wait_send()
    for copy in results:
        copy.wait()


def combine(
    clus, probe, density_in, z_hbm, f_hbm, fill_hbm, density_out, filling_out, forces_out,
    z_in, f_in, fill_in, forces, filling, sems,
):
    me = lax.axis_index("clus")
    has_far = jnp.logical_and(me > 0, me < clus - 1)
    arrivals = ((z_hbm, z_in), (fill_hbm, fill_in), (density_in, density_out))
    z_copy, fill_copy, density_copy = [
        pltpu.make_async_copy(source, target, sems.at[i]) for i, (source, target) in enumerate(arrivals)
    ]
    f_copy = pltpu.make_async_copy(f_hbm, f_in, sems.at[3])

    @pl.when(has_far)
    def _():
        f_copy.start()

    @pl.when(jnp.logical_not(has_far))
    def _():
        f_in[...] = jnp.zeros(f_in.shape, F32)

    z_copy.start()
    fill_copy.start()
    density_copy.start()

    @pl.when(has_far)
    def _():
        f_copy.wait()

    z_copy.wait()
    summed = z_in[0]
    for q in range(1, probe):
        summed = summed + z_in[q]
    for q in range(probe):
        summed = summed + f_in[q]
    for quad in range(CL // 4):
        forces[:, quad * B : (quad + 1) * B] = summed[quad * 3 : quad * 3 + 3]
    forces_copy = pltpu.make_async_copy(forces, forces_out, sems.at[4])
    forces_copy.start()
    fill_copy.wait()
    filled = fill_in[0]
    for q in range(1, clus):
        filled = filled + fill_in[q]
    filling[0] = jnp.sum(filled) / (clus * CL * B)
    filling_copy = pltpu.make_async_copy(filling, filling_out, sems.at[5])
    filling_copy.start()
    density_copy.wait()
    forces_copy.wait()
    filling_copy.wait()


def cosines():
    angles = np.pi * (np.arange(QUAD_NODES) + 0.5) / QUAD_NODES
    table = np.zeros((8, B), np.float32)
    for k in range(ORDER + 1):
        table[k, :QUAD_NODES] = np.cos(k * angles)
    return table


def solution(mesh):
    clus, probe = mesh.shape["clus"], mesh.shape["probe"]
    small = 1 + clus // 2
    vmem, dma = pltpu.VMEM, pltpu.SemaphoreType.DMA

    def local(probes, onsite, hopping, block_col, atom_of, bond_dir, chemical_potential):
        in_hbm = pl.BlockSpec(memory_space=pltpu.HBM)
        shapes = (
            jax.ShapeDtypeStruct((CL, B), F32),
            jax.ShapeDtypeStruct((1,), F32),
            jax.ShapeDtypeStruct((3, CL * ATOMS), F32),
        )
        found = pl.pallas_call(
            functools.partial(kernel, clus, probe),
            out_shape=(
                jax.ShapeDtypeStruct((CL, B), F32),
                jax.ShapeDtypeStruct((probe, 16, B), F32),
                jax.ShapeDtypeStruct((probe, 16, B), F32),
                jax.ShapeDtypeStruct((clus, 8, B), F32),
            ),
            in_specs=[in_hbm] * 8,
            out_specs=(in_hbm,) * 4,
            scratch_shapes=[
                vmem((CL, B), F32),
                pltpu.SMEM((1,), F32),
                vmem((CL, ROWS, B), BF16),
                vmem((CL, B), F32),
                vmem((CL, SLOTS), jnp.int32),
                vmem((CL, B), jnp.int32),
                vmem((3, CL, SLOTS), BF16),
                vmem((8, B), F32),
                vmem((CL, B), jnp.int32),
                vmem((EMPTY + 1, B, B), BF16),
                vmem((EMPTY + 1, B, B), BF16),
                vmem((16, B), jnp.int32),
                vmem((48, B), F32),
                pltpu.SMEM((16, B), jnp.int32),
                pltpu.SMEM((48, B), F32),
                vmem((ORDER + 1, CL, ROWS, B), BF16),
                vmem((ORDER + 1, 2, CL, ROWS, B), BF16),
                vmem((ORDER, 2, CL, ROWS, B), LINK),
                vmem((ORDER, 2, CL, ROWS, B), LINK),
                vmem((2, CL, ROWS, B), F32),
                vmem((CL, ROWS, B), F32),
                vmem((CL, ROWS, B), F32),
                vmem((8, B), F32),
                vmem((3, ROWS, B), F32),
                vmem((small, ROWS, B), F32),
                vmem((8, B), F32),
                vmem((16, B), F32),
                vmem((probe, 16, B), F32),
                vmem((CL, 3, 8, B), F32),
                vmem((CL, 3, 8, B), F32),
                vmem((CL * (CL + 1) // 2, 2 * ROWS, B), F32),
                vmem((40, B), F32),
                vmem((40, B), F32),
                vmem((2, CL, B, B), BF16),
                vmem((16, B), F32),
                vmem((16, B), F32),
                dma((7,)),
                dma((3,)),
                dma((SLOTS,)),
                dma((2,)),
                dma((2,)),
                dma((ORDER + 1, 2)),
                dma((ORDER + 1, 2)),
                dma((ORDER, 2)),
                dma((ORDER, 2)),
                dma((small,)),
                dma((small,)),
                dma((clus,)),
                dma((clus,)),
                dma((probe,)),
                dma((probe,)),
                dma((1,)),
                dma((1,)),
                dma((probe,)),
                dma((probe,)),
                dma((probe,)),
                dma((probe,)),
                pltpu.SemaphoreType.REGULAR((4,)),
            ],
            compiler_params=pltpu.CompilerParams(
                collective_id=0, has_side_effects=True, vmem_limit_bytes=60 * 1024 * 1024
            ),
            cost_estimate=pl.CostEstimate(flops=2_600_000_000, bytes_accessed=8_500_000, transcendentals=0),
            name="fermi_forces",
        )(
            probes, onsite, hopping, block_col.T, atom_of, jnp.swapaxes(bond_dir, 1, 2), chemical_potential,
            jnp.asarray(cosines()),
        )
        return pl.pallas_call(
            functools.partial(combine, clus, probe),
            out_shape=shapes,
            in_specs=[in_hbm] * 4,
            out_specs=(in_hbm,) * 3,
            scratch_shapes=[
                vmem((probe, 16, B), F32),
                vmem((probe, 16, B), F32),
                vmem((clus, 8, B), F32),
                vmem((3, CL * ATOMS), F32),
                pltpu.SMEM((1,), F32),
                dma((6,)),
            ],
            compiler_params=pltpu.CompilerParams(vmem_limit_bytes=60 * 1024 * 1024),
            name="combine",
        )(*found)

    return jax.shard_map(
        local,
        mesh=mesh,
        in_specs=(
            P("clus", "probe", None),
            P("clus", None),
            P(None, "clus", None, None),
            P(None, "clus"),
            P("clus", None),
            P(None, None, "clus"),
            P(),
        ),
        out_specs=(P("clus", None), P(), P(None, "clus")),
        check_vma=False,
    )
```

```python
import functools

import jax
import jax.numpy as jnp
import numpy as np
from jax import lax
from jax.experimental import pallas as pl
from jax.experimental.pallas import tpu as pltpu
from jax.sharding import PartitionSpec as P

MESH = pl.DeviceIdType.MESH
CL = 12
SLOTS = 20
ROWS = 16
B = 128
CHIPS_Y = 4
ATOMS = 32
REACH = 12
ORDER = 4
PROBE_VECTORS = 128
DECAY = 50.0
SMEARING_TEMP = 0.1
QUAD_NODES = 64
EMPTY = CL * SLOTS
F32 = jnp.float32
BF16 = jnp.bfloat16
FAR, NEAR = 0, 1
LINK = BF16


def pair_offset(side, own, other):
    if side == FAR:
        return REACH - 1 - other - own if other + own <= REACH - 1 else None
    return 3 * REACH - 1 - other - own if other + own >= REACH - 1 else None


def kernel(
    clus, probe, probes_hbm, onsite_hbm, hop_ref, col_hbm, atom_hbm, bond_hbm, mu_hbm, cos_hbm,
    density_hbm, z_in, f_in, fill_in,
    density_ref, mu_ref, probes_ref, onsite_ref, col_ref, atom_ref, bond_ref, cos_ref, atom_far, kbuf, ktbuf, tab_v, bond_v, tab, bond, xs, halo, part_out, part_in, cheb, fermi, y_acc, coef,
    norm_buf, norm_in, fill_buf, dens_out, dens_in, force_acc, far_acc, ahead, col_out, col_in, onehot, z_out, f_out,
    isem, osem, ksem, tsem, asem, hs, hr, ps, pr, ns, nr, gs, gr, ds, dr, fs, fr, zs, zr, ws, wr, word,
):
    me = lax.axis_index("clus")
    z = lax.axis_index("probe")
    flip = me % 2
    sign = 1 - 2 * flip
    place = [flip * (CL - 1) + sign * c for c in range(CL)]
    chips = clus // 2
    chip = me // 2
    has_far = jnp.logical_and(me > 0, me < clus - 1)

    far_clus = (me + clus - sign) % clus
    far = (far_clus, z)
    near = (me + sign, z)
    chip_peers = [(((chip + q) % chips) * 2 + flip, z) for q in range(1, chips)]
    z_peers = [(me, (z + q) % probe) for q in range(1, probe)]
    far_peers = [(far_clus, (z + q) % probe) for q in range(probe)]

    chips_x = chips // CHIPS_Y
    cx, cy = chip // CHIPS_Y, chip % CHIPS_Y
    along_x = [((((cx + q) % chips_x) * CHIPS_Y + cy) * 2 + flip, z) for q in (1, chips_x - 1)]
    along_y = [((cx * CHIPS_Y + (cy + q) % CHIPS_Y) * 2 + flip, z) for q in (1, CHIPS_Y - 1)]
    along_z = [(me, (z + q) % probe) for q in (1, probe - 1)]
    rounds = [along_z + along_y, along_z + along_y, along_z + along_x, along_z + along_x]

    def spread(i):
        for peer in rounds[i]:
            pl.semaphore_signal(word.at[i], inc=1, device_id=peer, device_id_type=MESH)

    def heard(i):
        pl.semaphore_wait(word.at[i], len(rounds[i]))

    barrier = pltpu.get_barrier_semaphore()
    everyone = [near] + along_x + along_y + along_z
    for peer in everyone:
        pl.semaphore_signal(barrier, inc=1, device_id=peer, device_id_type=MESH)

    @pl.when(has_far)
    def _():
        pl.semaphore_signal(barrier, inc=1, device_id=far, device_id_type=MESH)

    def send(src, dst, s, r, peer):
        return pltpu.make_async_remote_copy(
            src_ref=src, dst_ref=dst, send_sem=s, recv_sem=r, device_id=peer, device_id_type=MESH
        )

    loads = [
        pltpu.make_async_copy(hop_ref.at[m], kbuf.at[pl.ds(m * CL, CL)], ksem.at[m]) for m in range(SLOTS)
    ]
    inputs = [
        pltpu.make_async_copy(source, target, isem.at[i])
        for i, (source, target) in enumerate(
            (
                (col_hbm, col_ref), (bond_hbm, bond_ref), (probes_hbm, probes_ref), (cos_hbm, cos_ref),
                (atom_hbm, atom_ref), (onsite_hbm, onsite_ref), (mu_hbm, mu_ref),
            )
        )
    ]
    for copy in inputs + loads:
        copy.start()
    for copy in inputs:
        copy.wait()

    lane = lax.broadcasted_iota(jnp.int32, (CL, SLOTS), 0)
    slot = lax.broadcasted_iota(jnp.int32, (CL, SLOTS), 1)
    columns = col_ref[...]
    rel = jnp.where(columns >= 0, columns - me * CL - lane + REACH, -1)
    rel = jnp.where(rel >= 0, rel * sign + flip * (2 * REACH), -1)
    flat = slot * CL + lane
    directions = [bond_ref[x].astype(F32) for x in range(3)]
    wide_lane = lax.broadcasted_iota(jnp.int32, (CL, B), 1)
    places = jnp.full((CL, B), EMPTY, jnp.int32)
    facing = [jnp.zeros((CL, B), F32)] * 3
    for o in range(2 * REACH + 1):
        hit = rel == o
        here = wide_lane == o
        places = jnp.where(here, jnp.min(jnp.where(hit, flat, EMPTY), axis=1, keepdims=True), places)
        for x in range(3):
            facing[x] = jnp.where(
                here, jnp.sum(jnp.where(hit, directions[x], 0.0), axis=1, keepdims=True), facing[x]
            )
    tab_v[0:CL, :] = places
    for x in range(3):
        bond_v[16 * x : 16 * x + CL, :] = facing[x]
    tables = [pltpu.make_async_copy(tab_v, tab, tsem.at[0]), pltpu.make_async_copy(bond_v, bond, tsem.at[1])]
    for copy in tables:
        copy.start()

    @pl.when(jnp.logical_not(has_far))
    def _():
        atom_far[...] = jnp.zeros(atom_far.shape, jnp.int32)
        halo[:, FAR] = jnp.zeros((ORDER + 1, CL, ROWS, B), BF16)
        part_in[:, FAR] = jnp.zeros((ORDER, CL, ROWS, B), LINK)

    nacc = jnp.zeros((ROWS, B), F32)
    for c in range(CL):
        xc = probes_ref[place[c]]
        xs[0, c] = xc
        wide = xc.astype(F32)
        cheb[0, c] = wide
        cheb[1, c] = jnp.zeros((ROWS, B), F32)
        nacc = nacc + wide * wide
    norm_buf[0] = nacc

    occupation = 1.0 / (1.0 + jnp.exp((cos_ref[1:2, :] - mu_ref[0]) / SMEARING_TEMP))
    weight = lax.broadcasted_iota(jnp.int32, (8, B), 0)
    total = jnp.sum(cos_ref[...] * occupation, axis=1, keepdims=True) * (2.0 / QUAD_NODES)
    coef[...] = jnp.broadcast_to(total, (8, B)) * jnp.where(weight == 0, 0.5, 1.0)
    for c in range(CL):
        fermi[c] = cheb[0, c] * coef[0:1, :]

    pl.semaphore_wait(barrier, len(everyone) + has_far.astype(jnp.int32))

    def halo_copy(k, side):
        return send(xs.at[k], halo.at[k, side], hs.at[k, side], hr.at[k, side], (far, near)[side])

    def part_copy(k, side):
        return send(part_out.at[k, side], part_in.at[k, side], ps.at[k, side], pr.at[k, side], (far, near)[side])

    def far_first(copies, first):
        order = sorted(range(len(copies)), key=lambda i: abs(i + first - probe // 2))
        return [copies[i] for i in order]

    def stage_copies(own, arrived, s, r, stage, arriving=False):
        if stage == 0:
            return [send(own.at[0], arrived.at[chips], s.at[0], r.at[chips], near)]
        copies = []
        for q, peer in enumerate(chip_peers):
            place_in = (chip + chips - q - 1) % chips if arriving else chip
            copies.append(send(own.at[stage], arrived.at[place_in], s.at[1 + q], r.at[place_in], peer))
        return copies

    norm_copies = functools.partial(stage_copies, norm_buf, norm_in, ns, nr)

    def fill_copies(arriving=False):
        copies = []
        for q in range(1, clus):
            place_in = (me + clus - q) % clus if arriving else me
            copies.append(send(fill_buf, fill_in.at[place_in], gs.at[q], gr.at[place_in], ((me + q) % clus, z)))
        return copies


    def collect(copies, own, arrived, stage):
        for copy in copies(stage, True):
            copy.wait_recv()
        if stage == 0:
            own[1] = own[0] + arrived[chips]
            return
        arrived[chip] = own[stage]
        value = arrived[0]
        for q in range(1, chips):
            value = value + arrived[q]
        own[stage + 1] = value

    def atoms_copy():
        return send(atom_ref, atom_far, asem.at[0], asem.at[1], far)

    @pl.when(has_far)
    def _():
        halo_copy(0, FAR).start()
        atoms_copy().start()

    halo_copy(0, NEAR).start()
    for copy in norm_copies(0):
        copy.start()
    spread(0)

    kbuf[EMPTY] = jnp.zeros((B, B), BF16)
    ktbuf[EMPTY] = jnp.zeros((B, B), BF16)

    for copy in loads + tables:
        copy.wait()

    def straight(o, c):
        return kbuf[tab[place[c], o]]

    def turned(o, c):
        return ktbuf[tab[place[c], o]]

    def product(vectors, blocks):
        return jnp.dot(
            jnp.concatenate(vectors, axis=1), jnp.concatenate(blocks, axis=0), preferred_element_type=F32
        )

    def side_direct(k, side, c):
        others = [b for b in range(CL) if pair_offset(side, c, b) is not None]
        return product(
            [halo[k, side, b] for b in others], [turned(pair_offset(side, c, b), c) for b in others]
        )

    def partials(k):
        x = [xs[k, c] for c in range(CL)]
        for side in (FAR, NEAR):
            for b in range(CL):
                own = [c for c in range(CL) if pair_offset(side, c, b) is not None]
                part_out[k, side, b] = product(
                    [x[c] for c in own], [straight(pair_offset(side, c, b), c) for c in own]
                ).astype(LINK)
            if side == FAR:

                @pl.when(has_far)
                def _():
                    part_copy(k, FAR).start()

            else:
                part_copy(k, NEAR).start()

    partials(0)

    def turn(m, carry):
        for i in range(5):
            for c in range(CL):
                ktbuf[(5 * m + i) * CL + c] = kbuf[(5 * m + i) * CL + c].T
        return carry

    lax.fori_loop(0, SLOTS // 5, turn, 0)
    collect(norm_copies, norm_buf, norm_in, 0)

    def apply(k, carry):
        @pl.when(jnp.logical_and(k >= 1, has_far))
        def _():
            halo_copy(k, FAR).start()

        @pl.when(k >= 1)
        def _():
            halo_copy(k, NEAR).start()

        @pl.when(k >= 1)
        def _():
            partials(k)

        x = [xs[k, c] for c in range(CL)]
        for c in range(CL):
            y_acc[c] = product(
                x + x,
                [turned(REACH + d - c, c) for d in range(CL)] + [straight(REACH + c - d, d) for d in range(CL)],
            )

        @pl.when(k == 0)
        def _():
            heard(0)
            spread(1)

        @pl.when(k == 1)
        def _():
            heard(1)
            spread(2)

        @pl.when(k == 2)
        def _():
            heard(2)
            spread(3)
            for copy in norm_copies(1):
                copy.start()

        @pl.when(k == 3)
        def _():
            heard(3)

        halo_copy(k, NEAR).wait_recv()
        for c in range(CL):
            y_acc[c] = y_acc[c] + side_direct(k, NEAR, c)
        part_copy(k, NEAR).wait_recv()

        @pl.when(has_far)
        def _():
            halo_copy(k, FAR).wait_recv()

        for c in range(CL):
            y_acc[c] = y_acc[c] + part_in[k, NEAR, c].astype(F32) + side_direct(k, FAR, c)

        @pl.when(has_far)
        def _():
            part_copy(k, FAR).wait_recv()

        alpha = jnp.where(k == 0, 1.0, 2.0)
        into = (k + 1) % 2
        for c in range(CL):
            image = y_acc[c] + part_in[k, FAR, c].astype(F32)
            image = image + onsite_ref[pl.ds(place[c], 1), :] * xs[k, c].astype(F32)
            following = alpha * image - cheb[into, c]
            cheb[into, c] = following
            fermi[c] = fermi[c] + coef[pl.ds(k + 1, 1), :] * following
            xs[k + 1, c] = following.astype(BF16)
        return carry

    lax.fori_loop(0, ORDER, apply, 0)

    collect(norm_copies, norm_buf, norm_in, 1)
    norm_sq = jnp.sum(norm_buf[2], axis=1, keepdims=True)
    scale = jnp.broadcast_to((clus * CL * B) / (norm_sq * PROBE_VECTORS), (ROWS, B))
    for c in range(CL):
        scaled = fermi[c] * scale
        fermi[c] = scaled
        xs[ORDER, c] = scaled.astype(BF16)

    @pl.when(has_far)
    def _():
        halo_copy(ORDER, FAR).start()

    halo_copy(ORDER, NEAR).start()
    dens_out[...] = jnp.zeros(dens_out.shape, F32)
    for c in range(CL):
        row = jnp.sum(xs[0, c].astype(F32) * fermi[c], axis=0, keepdims=True)
        dens_out[c : c + 1, :] = row

    def z_copies(src, dst, s, r, arriving=False):
        copies = []
        for q, peer in enumerate(z_peers):
            slot = (z + probe - q - 1) % probe if arriving else z
            copies.append(send(src, dst.at[slot], s.at[q], r.at[slot], peer))
        return far_first(copies, 1)

    def z_sum(src, dst, s, r):
        dst[z] = src[...]
        for copy in z_copies(src, dst, s, r, True):
            copy.wait_recv()
        value = dst[0]
        for q in range(1, probe):
            value = value + dst[q]
        return value

    for copy in z_copies(dens_out, dens_in, ds, dr):
        copy.start()

    far_pairs = [(c, b) for b in range(CL) for c in range(CL) if pair_offset(FAR, c, b) is not None]

    def sums(left, block, u, v):
        image = jnp.dot(left, block, preferred_element_type=F32)
        r = v * image[:ROWS] + u * image[ROWS:]
        return r[:8] + r[8:]

    both = [jnp.concatenate([xs[0, c], xs[ORDER, c]], axis=0) for c in range(CL)]

    def own_vectors(c):
        return xs[0, c].astype(F32), xs[ORDER, c].astype(F32)

    def add(acc, o, c, r, positive):
        out = []
        for x in range(3):
            term = bond[16 * x + place[c], o] * r
            out.append(acc[x] + term if positive else acc[x] - term)
        return out

    zero3 = [jnp.zeros((8, B), F32)] * 3
    for c in range(CL):
        u, v = own_vectors(c)
        acc = zero3
        for d in range(CL):
            o = REACH + d - c
            acc = add(acc, o, c, sums(both[d], turned(o, c), u, v), False)
        for d in range(CL):
            o = REACH + c - d
            acc = add(acc, o, d, sums(both[d], straight(o, d), u, v), True)
        for x in range(3):
            force_acc[c, x] = acc[x]

    def col_copy():
        return send(col_out, col_in, fs.at[0], fr.at[0], near)

    row = lax.broadcasted_iota(jnp.int32, (B, B), 0)

    @pl.when(has_far)
    def _():
        atoms_copy().wait_recv()

    for c in range(CL):
        onehot[0, c] = (row == atom_ref[c : c + 1, :] + ATOMS * (c % 4)).astype(BF16)
        onehot[1, c] = (row == atom_far[c : c + 1, :] + ATOMS * (c % 4)).astype(BF16)

    dims = (((1,), (1,)), ((), ()))
    pick = lax.broadcasted_iota(jnp.int32, (8, B), 0)

    def atom_sums(which, source, target):
        for quad in range(CL // 4):
            pieces = []
            for c in range(quad * 4, quad * 4 + 4):
                value = jnp.where(pick == 0, source(c, 0), jnp.where(pick == 1, source(c, 1), source(c, 2)))
                high = value.astype(BF16).astype(F32)
                rest = value - high
                middle = rest.astype(BF16).astype(F32)
                pieces.append(jnp.concatenate([high, middle, rest - middle, jnp.zeros((8, B), F32)], axis=0).astype(BF16))
            owners = jnp.concatenate([onehot[which, c] for c in range(quad * 4, quad * 4 + 4)], axis=1)
            total = lax.dot_general(jnp.concatenate(pieces, axis=1), owners, dims, preferred_element_type=F32)
            total = total[0:8] + total[8:16] + total[16:24]
            target[quad * 3 : quad * 3 + 3, :] = total[0:3]

    def far_copies(arriving=False):
        copies = []
        for q, peer in enumerate(far_peers):
            place_in = (z + probe - q) % probe if arriving else z
            copies.append(send(f_out, f_in.at[place_in], ws.at[q], wr.at[place_in], peer))
        return far_first(copies, 0)

    def halo_both(side, b):
        return jnp.concatenate([halo[0, side, b], halo[ORDER, side, b]], axis=0)

    z_out[...] = jnp.zeros(z_out.shape, F32)
    f_out[...] = jnp.zeros(f_out.shape, F32)
    for side in (NEAR, FAR):
        if side == NEAR:
            halo_copy(ORDER, NEAR).wait_recv()
        else:
            for i, (c, b) in enumerate(far_pairs):
                ahead[i] = jnp.dot(both[c], straight(pair_offset(FAR, c, b), c), preferred_element_type=F32)

            @pl.when(has_far)
            def _():
                halo_copy(ORDER, FAR).wait_recv()

        for b in range(CL):
            u, v = halo[0, side, b].astype(F32), halo[ORDER, side, b].astype(F32)
            acc = zero3
            for c in range(CL):
                o = pair_offset(side, c, b)
                if o is not None and side == NEAR:
                    acc = add(acc, o, c, sums(both[c], straight(o, c), u, v), True)
                elif o is not None:
                    image = ahead[far_pairs.index((c, b))]
                    r = v * image[:ROWS] + u * image[ROWS:]
                    acc = add(acc, o, c, r[:8] + r[8:], True)
            for x in range(3):
                total = jnp.sum(acc[x], axis=0, keepdims=True)
                if side == NEAR:
                    col_out[3 * b + x : 3 * b + x + 1, :] = total
                else:
                    far_acc[b, x] = jnp.broadcast_to(total * DECAY, (8, B))
        if side == NEAR:
            col_copy().start()
        else:
            atom_sums(1, lambda c, x: far_acc[(1 - flip) * (CL - 1) - sign * c, x], f_out)

            @pl.when(has_far)
            def _():
                for copy in far_copies():
                    copy.start()

        for c in range(CL):
            u, v = own_vectors(c)
            acc = [force_acc[c, x] for x in range(3)]
            for b in range(CL):
                o = pair_offset(side, c, b)
                if o is not None:
                    acc = add(acc, o, c, sums(halo_both(side, b), turned(o, c), u, v), False)
            for x in range(3):
                force_acc[c, x] = acc[x]

    col_copy().wait_recv()
    for c in range(CL):
        for x in range(3):
            j = 3 * c + x
            value = jnp.sum(force_acc[c, x], axis=0, keepdims=True) + col_in[j : j + 1, :]
            force_acc[c, x] = jnp.broadcast_to(value * DECAY, (8, B))
    atom_sums(0, lambda c, x: force_acc[place[c], x], z_out)
    for copy in z_copies(z_out, z_in, zs, zr):
        copy.start()

    summed = z_sum(dens_out, dens_in, ds, dr)
    for c in range(CL):
        density_ref[pl.ds(place[c], 1), :] = summed[c : c + 1, :]
    fill_buf[...] = summed[0:8] + summed[8:16]
    for copy in fill_copies():
        copy.start()
    results = [
        pltpu.make_async_copy(source, target, osem.at[i])
        for i, (source, target) in enumerate(
            ((density_ref, density_hbm), (fill_buf, fill_in.at[me]), (z_out, z_in.at[z]))
        )
    ]
    for copy in results:
        copy.start()

    @pl.when(has_far)
    def _():
        for copy in far_copies(True):
            copy.wait_recv()

    for copy in z_copies(z_out, z_in, zs, zr, True) + fill_copies(True):
        copy.wait_recv()

    def finish(k, carry):
        halo_copy(k, NEAR).wait_send()
        part_copy(k, NEAR).wait_send()

        @pl.when(has_far)
        def _():
            halo_copy(k, FAR).wait_send()
            part_copy(k, FAR).wait_send()

        return carry

    lax.fori_loop(0, ORDER, finish, 0)
    halo_copy(ORDER, NEAR).wait_send()
    col_copy().wait_send()

    @pl.when(has_far)
    def _():
        halo_copy(ORDER, FAR).wait_send()
        atoms_copy().wait_send()
        for copy in far_copies():
            copy.wait_send()

    for stage in range(2):
        for copy in norm_copies(stage):
            copy.wait_send()
    for copy in fill_copies():
        copy.wait_send()
    for copy in z_copies(dens_out, dens_in, ds, dr) + z_copies(z_out, z_in, zs, zr):
        copy.wait_send()
    for copy in results:
        copy.wait()


def combine(
    clus, probe, density_in, z_hbm, f_hbm, fill_hbm, density_out, filling_out, forces_out,
    z_in, f_in, fill_in, forces, filling, sems,
):
    me = lax.axis_index("clus")
    has_far = jnp.logical_and(me > 0, me < clus - 1)
    arrivals = ((z_hbm, z_in), (fill_hbm, fill_in), (density_in, density_out))
    z_copy, fill_copy, density_copy = [
        pltpu.make_async_copy(source, target, sems.at[i]) for i, (source, target) in enumerate(arrivals)
    ]
    f_copy = pltpu.make_async_copy(f_hbm, f_in, sems.at[3])

    @pl.when(has_far)
    def _():
        f_copy.start()

    @pl.when(jnp.logical_not(has_far))
    def _():
        f_in[...] = jnp.zeros(f_in.shape, F32)

    z_copy.start()
    fill_copy.start()
    density_copy.start()

    @pl.when(has_far)
    def _():
        f_copy.wait()

    z_copy.wait()
    summed = z_in[0]
    for q in range(1, probe):
        summed = summed + z_in[q]
    for q in range(probe):
        summed = summed + f_in[q]
    for quad in range(CL // 4):
        forces[:, quad * B : (quad + 1) * B] = summed[quad * 3 : quad * 3 + 3]
    forces_copy = pltpu.make_async_copy(forces, forces_out, sems.at[4])
    forces_copy.start()
    fill_copy.wait()
    filled = fill_in[0]
    for q in range(1, clus):
        filled = filled + fill_in[q]
    filling[0] = jnp.sum(filled) / (clus * CL * B)
    filling_copy = pltpu.make_async_copy(filling, filling_out, sems.at[5])
    filling_copy.start()
    density_copy.wait()
    forces_copy.wait()
    filling_copy.wait()


def cosines():
    angles = np.pi * (np.arange(QUAD_NODES) + 0.5) / QUAD_NODES
    table = np.zeros((8, B), np.float32)
    for k in range(ORDER + 1):
        table[k, :QUAD_NODES] = np.cos(k * angles)
    return table


def solution(mesh):
    clus, probe = mesh.shape["clus"], mesh.shape["probe"]
    small = 1 + clus // 2
    vmem, dma = pltpu.VMEM, pltpu.SemaphoreType.DMA

    def local(probes, onsite, hopping, block_col, atom_of, bond_dir, chemical_potential):
        in_hbm = pl.BlockSpec(memory_space=pltpu.HBM)
        shapes = (
            jax.ShapeDtypeStruct((CL, B), F32),
            jax.ShapeDtypeStruct((1,), F32),
            jax.ShapeDtypeStruct((3, CL * ATOMS), F32),
        )
        found = pl.pallas_call(
            functools.partial(kernel, clus, probe),
            out_shape=(
                jax.ShapeDtypeStruct((CL, B), F32),
                jax.ShapeDtypeStruct((probe, 16, B), F32),
                jax.ShapeDtypeStruct((probe, 16, B), F32),
                jax.ShapeDtypeStruct((clus, 8, B), F32),
            ),
            in_specs=[in_hbm] * 8,
            out_specs=(in_hbm,) * 4,
            scratch_shapes=[
                vmem((CL, B), F32),
                pltpu.SMEM((1,), F32),
                vmem((CL, ROWS, B), BF16),
                vmem((CL, B), F32),
                vmem((CL, SLOTS), jnp.int32),
                vmem((CL, B), jnp.int32),
                vmem((3, CL, SLOTS), BF16),
                vmem((8, B), F32),
                vmem((CL, B), jnp.int32),
                vmem((EMPTY + 1, B, B), BF16),
                vmem((EMPTY + 1, B, B), BF16),
                vmem((16, B), jnp.int32),
                vmem((48, B), F32),
                pltpu.SMEM((16, B), jnp.int32),
                pltpu.SMEM((48, B), F32),
                vmem((ORDER + 1, CL, ROWS, B), BF16),
                vmem((ORDER + 1, 2, CL, ROWS, B), BF16),
                vmem((ORDER, 2, CL, ROWS, B), LINK),
                vmem((ORDER, 2, CL, ROWS, B), LINK),
                vmem((2, CL, ROWS, B), F32),
                vmem((CL, ROWS, B), F32),
                vmem((CL, ROWS, B), F32),
                vmem((8, B), F32),
                vmem((3, ROWS, B), F32),
                vmem((small, ROWS, B), F32),
                vmem((8, B), F32),
                vmem((16, B), F32),
                vmem((probe, 16, B), F32),
                vmem((CL, 3, 8, B), F32),
                vmem((CL, 3, 8, B), F32),
                vmem((CL * (CL + 1) // 2, 2 * ROWS, B), F32),
                vmem((40, B), F32),
                vmem((40, B), F32),
                vmem((2, CL, B, B), BF16),
                vmem((16, B), F32),
                vmem((16, B), F32),
                dma((7,)),
                dma((3,)),
                dma((SLOTS,)),
                dma((2,)),
                dma((2,)),
                dma((ORDER + 1, 2)),
                dma((ORDER + 1, 2)),
                dma((ORDER, 2)),
                dma((ORDER, 2)),
                dma((small,)),
                dma((small,)),
                dma((clus,)),
                dma((clus,)),
                dma((probe,)),
                dma((probe,)),
                dma((1,)),
                dma((1,)),
                dma((probe,)),
                dma((probe,)),
                dma((probe,)),
                dma((probe,)),
                pltpu.SemaphoreType.REGULAR((4,)),
            ],
            compiler_params=pltpu.CompilerParams(
                collective_id=0, has_side_effects=True, vmem_limit_bytes=60 * 1024 * 1024
            ),
            cost_estimate=pl.CostEstimate(flops=2_600_000_000, bytes_accessed=8_500_000, transcendentals=0),
            name="fermi_forces",
        )(
            probes, onsite, hopping, block_col.T, atom_of, jnp.swapaxes(bond_dir, 1, 2), chemical_potential,
            jnp.asarray(cosines()),
        )
        return pl.pallas_call(
            functools.partial(combine, clus, probe),
            out_shape=shapes,
            in_specs=[in_hbm] * 4,
            out_specs=(in_hbm,) * 3,
            scratch_shapes=[
                vmem((probe, 16, B), F32),
                vmem((probe, 16, B), F32),
                vmem((clus, 8, B), F32),
                vmem((3, CL * ATOMS), F32),
                pltpu.SMEM((1,), F32),
                dma((6,)),
            ],
            compiler_params=pltpu.CompilerParams(vmem_limit_bytes=60 * 1024 * 1024),
            name="combine",
        )(*found)

    return jax.shard_map(
        local,
        mesh=mesh,
        in_specs=(
            P("clus", "probe", None),
            P("clus", None),
            P(None, "clus", None, None),
            P(None, "clus"),
            P("clus", None),
            P(None, None, "clus"),
            P(),
        ),
        out_specs=(P("clus", None), P(), P(None, "clus")),
        check_vma=False,
    )
```

```python
import functools

import jax
import jax.numpy as jnp
import numpy as np
from jax import lax
from jax.experimental import pallas as pl
from jax.experimental.pallas import tpu as pltpu
from jax.sharding import PartitionSpec as P

MESH = pl.DeviceIdType.MESH
CL = 12
SLOTS = 20
ROWS = 16
B = 128
CHIPS_Y = 4
ATOMS = 32
REACH = 12
ORDER = 4
PROBE_VECTORS = 128
DECAY = 50.0
SMEARING_TEMP = 0.1
QUAD_NODES = 64
EMPTY = CL * SLOTS
F32 = jnp.float32
BF16 = jnp.bfloat16
FAR, NEAR = 0, 1
LINK = BF16


def pair_offset(side, own, other):
    if side == FAR:
        return REACH - 1 - other - own if other + own <= REACH - 1 else None
    return 3 * REACH - 1 - other - own if other + own >= REACH - 1 else None


def kernel(
    clus, probe, probes_hbm, onsite_hbm, hop_ref, col_hbm, atom_hbm, bond_hbm, mu_hbm, cos_hbm,
    density_hbm, z_in, f_in, fill_in,
    density_ref, mu_ref, probes_ref, onsite_ref, col_ref, atom_ref, bond_ref, cos_ref, atom_far, kbuf, ktbuf, tab_v, bond_v, tab, bond, xs, halo, part_out, part_in, cheb, fermi, y_acc, coef,
    norm_buf, norm_in, fill_buf, dens_out, dens_in, force_acc, far_acc, ahead, col_out, col_in, onehot, z_out, f_out,
    isem, osem, ksem, tsem, asem, hs, hr, ps, pr, ns, nr, gs, gr, ds, dr, fs, fr, zs, zr, ws, wr, word,
):
    me = lax.axis_index("clus")
    z = lax.axis_index("probe")
    flip = me % 2
    sign = 1 - 2 * flip
    place = [flip * (CL - 1) + sign * c for c in range(CL)]
    chips = clus // 2
    chip = me // 2
    has_far = jnp.logical_and(me > 0, me < clus - 1)

    far_clus = (me + clus - sign) % clus
    far = (far_clus, z)
    near = (me + sign, z)
    chip_peers = [(((chip + q) % chips) * 2 + flip, z) for q in range(1, chips)]
    z_peers = [(me, (z + q) % probe) for q in range(1, probe)]
    far_peers = [(far_clus, (z + q) % probe) for q in range(probe)]

    chips_x = chips // CHIPS_Y
    cx, cy = chip // CHIPS_Y, chip % CHIPS_Y
    along_x = [((((cx + q) % chips_x) * CHIPS_Y + cy) * 2 + flip, z) for q in (1, chips_x - 1)]
    along_y = [((cx * CHIPS_Y + (cy + q) % CHIPS_Y) * 2 + flip, z) for q in (1, CHIPS_Y - 1)]
    along_z = [(me, (z + q) % probe) for q in (1, probe - 1)]
    rounds = [along_z + along_y, along_z + along_y, along_z + along_x, along_z + along_x]

    def spread(i):
        for peer in rounds[i]:
            pl.semaphore_signal(word.at[i], inc=1, device_id=peer, device_id_type=MESH)

    def heard(i):
        pl.semaphore_wait(word.at[i], len(rounds[i]))

    barrier = pltpu.get_barrier_semaphore()
    everyone = [near] + along_x + along_y + along_z
    for peer in everyone:
        pl.semaphore_signal(barrier, inc=1, device_id=peer, device_id_type=MESH)

    @pl.when(has_far)
    def _():
        pl.semaphore_signal(barrier, inc=1, device_id=far, device_id_type=MESH)

    def send(src, dst, s, r, peer):
        return pltpu.make_async_remote_copy(
            src_ref=src, dst_ref=dst, send_sem=s, recv_sem=r, device_id=peer, device_id_type=MESH
        )

    loads = [
        pltpu.make_async_copy(hop_ref.at[m], kbuf.at[pl.ds(m * CL, CL)], ksem.at[m]) for m in range(SLOTS)
    ]
    inputs = [
        pltpu.make_async_copy(source, target, isem.at[i])
        for i, (source, target) in enumerate(
            (
                (col_hbm, col_ref), (bond_hbm, bond_ref), (probes_hbm, probes_ref), (cos_hbm, cos_ref),
                (atom_hbm, atom_ref), (onsite_hbm, onsite_ref), (mu_hbm, mu_ref),
            )
        )
    ]
    for copy in inputs + loads:
        copy.start()
    for copy in inputs:
        copy.wait()

    lane = lax.broadcasted_iota(jnp.int32, (CL, SLOTS), 0)
    slot = lax.broadcasted_iota(jnp.int32, (CL, SLOTS), 1)
    columns = col_ref[...]
    rel = jnp.where(columns >= 0, columns - me * CL - lane + REACH, -1)
    rel = jnp.where(rel >= 0, rel * sign + flip * (2 * REACH), -1)
    flat = slot * CL + lane
    directions = [bond_ref[x].astype(F32) for x in range(3)]
    wide_lane = lax.broadcasted_iota(jnp.int32, (CL, B), 1)
    places = jnp.full((CL, B), EMPTY, jnp.int32)
    facing = [jnp.zeros((CL, B), F32)] * 3
    for o in range(2 * REACH + 1):
        hit = rel == o
        here = wide_lane == o
        places = jnp.where(here, jnp.min(jnp.where(hit, flat, EMPTY), axis=1, keepdims=True), places)
        for x in range(3):
            facing[x] = jnp.where(
                here, jnp.sum(jnp.where(hit, directions[x], 0.0), axis=1, keepdims=True), facing[x]
            )
    tab_v[0:CL, :] = places
    for x in range(3):
        bond_v[16 * x : 16 * x + CL, :] = facing[x]
    tables = [pltpu.make_async_copy(tab_v, tab, tsem.at[0]), pltpu.make_async_copy(bond_v, bond, tsem.at[1])]
    for copy in tables:
        copy.start()

    @pl.when(jnp.logical_not(has_far))
    def _():
        atom_far[...] = jnp.zeros(atom_far.shape, jnp.int32)
        halo[:, FAR] = jnp.zeros((ORDER + 1, CL, ROWS, B), BF16)
        part_in[:, FAR] = jnp.zeros((ORDER, CL, ROWS, B), LINK)

    nacc = jnp.zeros((ROWS, B), F32)
    for c in range(CL):
        xc = probes_ref[place[c]]
        xs[0, c] = xc
        wide = xc.astype(F32)
        cheb[0, c] = wide
        cheb[1, c] = jnp.zeros((ROWS, B), F32)
        nacc = nacc + wide * wide
    norm_buf[0] = nacc

    occupation = 1.0 / (1.0 + jnp.exp((cos_ref[1:2, :] - mu_ref[0]) / SMEARING_TEMP))
    weight = lax.broadcasted_iota(jnp.int32, (8, B), 0)
    total = jnp.sum(cos_ref[...] * occupation, axis=1, keepdims=True) * (2.0 / QUAD_NODES)
    coef[...] = jnp.broadcast_to(total, (8, B)) * jnp.where(weight == 0, 0.5, 1.0)
    for c in range(CL):
        fermi[c] = cheb[0, c] * coef[0:1, :]

    pl.semaphore_wait(barrier, len(everyone) + has_far.astype(jnp.int32))

    def halo_copy(k, side):
        return send(xs.at[k], halo.at[k, side], hs.at[k, side], hr.at[k, side], (far, near)[side])

    def part_copy(k, side):
        return send(part_out.at[k, side], part_in.at[k, side], ps.at[k, side], pr.at[k, side], (far, near)[side])

    def far_first(copies, first):
        order = sorted(range(len(copies)), key=lambda i: abs(i + first - probe // 2))
        return [copies[i] for i in order]

    def stage_copies(own, arrived, s, r, stage, arriving=False):
        if stage == 0:
            return [send(own.at[0], arrived.at[chips], s.at[0], r.at[chips], near)]
        copies = []
        for q, peer in enumerate(chip_peers):
            place_in = (chip + chips - q - 1) % chips if arriving else chip
            copies.append(send(own.at[stage], arrived.at[place_in], s.at[1 + q], r.at[place_in], peer))
        return copies

    norm_copies = functools.partial(stage_copies, norm_buf, norm_in, ns, nr)

    def fill_copies(arriving=False):
        copies = []
        for q in range(1, clus):
            place_in = (me + clus - q) % clus if arriving else me
            copies.append(send(fill_buf, fill_in.at[place_in], gs.at[q], gr.at[place_in], ((me + q) % clus, z)))
        return copies


    def collect(copies, own, arrived, stage):
        for copy in copies(stage, True):
            copy.wait_recv()
        if stage == 0:
            own[1] = own[0] + arrived[chips]
            return
        arrived[chip] = own[stage]
        value = arrived[0]
        for q in range(1, chips):
            value = value + arrived[q]
        own[stage + 1] = value

    def atoms_copy():
        return send(atom_ref, atom_far, asem.at[0], asem.at[1], far)

    @pl.when(has_far)
    def _():
        halo_copy(0, FAR).start()
        atoms_copy().start()

    halo_copy(0, NEAR).start()
    for copy in norm_copies(0):
        copy.start()
    spread(0)

    kbuf[EMPTY] = jnp.zeros((B, B), BF16)
    ktbuf[EMPTY] = jnp.zeros((B, B), BF16)

    for copy in loads + tables:
        copy.wait()

    def straight(o, c):
        return kbuf[tab[place[c], o]]

    def turned(o, c):
        return ktbuf[tab[place[c], o]]

    def product(vectors, blocks):
        return jnp.dot(
            jnp.concatenate(vectors, axis=1), jnp.concatenate(blocks, axis=0), preferred_element_type=F32
        )

    def side_direct(k, side, c):
        others = [b for b in range(CL) if pair_offset(side, c, b) is not None]
        return product(
            [halo[k, side, b] for b in others], [turned(pair_offset(side, c, b), c) for b in others]
        )

    def partials(k):
        x = [xs[k, c] for c in range(CL)]
        for side in (FAR, NEAR):
            for b in range(CL):
                own = [c for c in range(CL) if pair_offset(side, c, b) is not None]
                part_out[k, side, b] = product(
                    [x[c] for c in own], [straight(pair_offset(side, c, b), c) for c in own]
                ).astype(LINK)
            if side == FAR:

                @pl.when(has_far)
                def _():
                    part_copy(k, FAR).start()

            else:
                part_copy(k, NEAR).start()

    partials(0)

    def turn(m, carry):
        for i in range(10):
            for c in range(CL):
                ktbuf[(10 * m + i) * CL + c] = kbuf[(10 * m + i) * CL + c].T
        return carry

    lax.fori_loop(0, SLOTS // 10, turn, 0)
    collect(norm_copies, norm_buf, norm_in, 0)

    def apply(k, carry):
        @pl.when(jnp.logical_and(k >= 1, has_far))
        def _():
            halo_copy(k, FAR).start()

        @pl.when(k >= 1)
        def _():
            halo_copy(k, NEAR).start()

        @pl.when(k >= 1)
        def _():
            partials(k)

        x = [xs[k, c] for c in range(CL)]
        for c in range(CL):
            y_acc[c] = product(
                x + x,
                [turned(REACH + d - c, c) for d in range(CL)] + [straight(REACH + c - d, d) for d in range(CL)],
            )

        @pl.when(k == 0)
        def _():
            heard(0)
            spread(1)

        @pl.when(k == 1)
        def _():
            heard(1)
            spread(2)

        @pl.when(k == 2)
        def _():
            heard(2)
            spread(3)
            for copy in norm_copies(1):
                copy.start()

        @pl.when(k == 3)
        def _():
            heard(3)

        halo_copy(k, NEAR).wait_recv()
        for c in range(CL):
            y_acc[c] = y_acc[c] + side_direct(k, NEAR, c)
        part_copy(k, NEAR).wait_recv()

        @pl.when(has_far)
        def _():
            halo_copy(k, FAR).wait_recv()

        for c in range(CL):
            y_acc[c] = y_acc[c] + part_in[k, NEAR, c].astype(F32) + side_direct(k, FAR, c)

        @pl.when(has_far)
        def _():
            part_copy(k, FAR).wait_recv()

        alpha = jnp.where(k == 0, 1.0, 2.0)
        into = (k + 1) % 2
        for c in range(CL):
            image = y_acc[c] + part_in[k, FAR, c].astype(F32)
            image = image + onsite_ref[pl.ds(place[c], 1), :] * xs[k, c].astype(F32)
            following = alpha * image - cheb[into, c]
            cheb[into, c] = following
            fermi[c] = fermi[c] + coef[pl.ds(k + 1, 1), :] * following
            xs[k + 1, c] = following.astype(BF16)
        return carry

    lax.fori_loop(0, ORDER, apply, 0)

    collect(norm_copies, norm_buf, norm_in, 1)
    norm_sq = jnp.sum(norm_buf[2], axis=1, keepdims=True)
    scale = jnp.broadcast_to((clus * CL * B) / (norm_sq * PROBE_VECTORS), (ROWS, B))
    for c in range(CL):
        scaled = fermi[c] * scale
        fermi[c] = scaled
        xs[ORDER, c] = scaled.astype(BF16)

    @pl.when(has_far)
    def _():
        halo_copy(ORDER, FAR).start()

    halo_copy(ORDER, NEAR).start()
    dens_out[...] = jnp.zeros(dens_out.shape, F32)
    for c in range(CL):
        row = jnp.sum(xs[0, c].astype(F32) * fermi[c], axis=0, keepdims=True)
        dens_out[c : c + 1, :] = row

    def z_copies(src, dst, s, r, arriving=False):
        copies = []
        for q, peer in enumerate(z_peers):
            slot = (z + probe - q - 1) % probe if arriving else z
            copies.append(send(src, dst.at[slot], s.at[q], r.at[slot], peer))
        return far_first(copies, 1)

    def z_sum(src, dst, s, r):
        dst[z] = src[...]
        for copy in z_copies(src, dst, s, r, True):
            copy.wait_recv()
        value = dst[0]
        for q in range(1, probe):
            value = value + dst[q]
        return value

    for copy in z_copies(dens_out, dens_in, ds, dr):
        copy.start()

    far_pairs = [(c, b) for b in range(CL) for c in range(CL) if pair_offset(FAR, c, b) is not None]

    def sums(left, block, u, v):
        image = jnp.dot(left, block, preferred_element_type=F32)
        r = v * image[:ROWS] + u * image[ROWS:]
        return r[:8] + r[8:]

    both = [jnp.concatenate([xs[0, c], xs[ORDER, c]], axis=0) for c in range(CL)]

    def own_vectors(c):
        return xs[0, c].astype(F32), xs[ORDER, c].astype(F32)

    def add(acc, o, c, r, positive):
        out = []
        for x in range(3):
            term = bond[16 * x + place[c], o] * r
            out.append(acc[x] + term if positive else acc[x] - term)
        return out

    zero3 = [jnp.zeros((8, B), F32)] * 3
    for c in range(CL):
        u, v = own_vectors(c)
        acc = zero3
        for d in range(CL):
            o = REACH + d - c
            acc = add(acc, o, c, sums(both[d], turned(o, c), u, v), False)
        for d in range(CL):
            o = REACH + c - d
            acc = add(acc, o, d, sums(both[d], straight(o, d), u, v), True)
        for x in range(3):
            force_acc[c, x] = acc[x]

    def col_copy():
        return send(col_out, col_in, fs.at[0], fr.at[0], near)

    row = lax.broadcasted_iota(jnp.int32, (B, B), 0)

    @pl.when(has_far)
    def _():
        atoms_copy().wait_recv()

    for c in range(CL):
        onehot[0, c] = (row == atom_ref[c : c + 1, :] + ATOMS * (c % 4)).astype(BF16)
        onehot[1, c] = (row == atom_far[c : c + 1, :] + ATOMS * (c % 4)).astype(BF16)

    dims = (((1,), (1,)), ((), ()))
    pick = lax.broadcasted_iota(jnp.int32, (8, B), 0)

    def atom_sums(which, source, target):
        for quad in range(CL // 4):
            pieces = []
            for c in range(quad * 4, quad * 4 + 4):
                value = jnp.where(pick == 0, source(c, 0), jnp.where(pick == 1, source(c, 1), source(c, 2)))
                high = value.astype(BF16).astype(F32)
                rest = value - high
                middle = rest.astype(BF16).astype(F32)
                pieces.append(jnp.concatenate([high, middle, rest - middle, jnp.zeros((8, B), F32)], axis=0).astype(BF16))
            owners = jnp.concatenate([onehot[which, c] for c in range(quad * 4, quad * 4 + 4)], axis=1)
            total = lax.dot_general(jnp.concatenate(pieces, axis=1), owners, dims, preferred_element_type=F32)
            total = total[0:8] + total[8:16] + total[16:24]
            target[quad * 3 : quad * 3 + 3, :] = total[0:3]

    def far_copies(arriving=False):
        copies = []
        for q, peer in enumerate(far_peers):
            place_in = (z + probe - q) % probe if arriving else z
            copies.append(send(f_out, f_in.at[place_in], ws.at[q], wr.at[place_in], peer))
        return far_first(copies, 0)

    def halo_both(side, b):
        return jnp.concatenate([halo[0, side, b], halo[ORDER, side, b]], axis=0)

    z_out[...] = jnp.zeros(z_out.shape, F32)
    f_out[...] = jnp.zeros(f_out.shape, F32)
    for side in (NEAR, FAR):
        if side == NEAR:
            halo_copy(ORDER, NEAR).wait_recv()
        else:
            for i, (c, b) in enumerate(far_pairs):
                ahead[i] = jnp.dot(both[c], straight(pair_offset(FAR, c, b), c), preferred_element_type=F32)

            @pl.when(has_far)
            def _():
                halo_copy(ORDER, FAR).wait_recv()

        for b in range(CL):
            u, v = halo[0, side, b].astype(F32), halo[ORDER, side, b].astype(F32)
            acc = zero3
            for c in range(CL):
                o = pair_offset(side, c, b)
                if o is not None and side == NEAR:
                    acc = add(acc, o, c, sums(both[c], straight(o, c), u, v), True)
                elif o is not None:
                    image = ahead[far_pairs.index((c, b))]
                    r = v * image[:ROWS] + u * image[ROWS:]
                    acc = add(acc, o, c, r[:8] + r[8:], True)
            for x in range(3):
                total = jnp.sum(acc[x], axis=0, keepdims=True)
                if side == NEAR:
                    col_out[3 * b + x : 3 * b + x + 1, :] = total
                else:
                    far_acc[b, x] = jnp.broadcast_to(total * DECAY, (8, B))
        if side == NEAR:
            col_copy().start()
        else:
            atom_sums(1, lambda c, x: far_acc[(1 - flip) * (CL - 1) - sign * c, x], f_out)

            @pl.when(has_far)
            def _():
                for copy in far_copies():
                    copy.start()

        for c in range(CL):
            u, v = own_vectors(c)
            acc = [force_acc[c, x] for x in range(3)]
            for b in range(CL):
                o = pair_offset(side, c, b)
                if o is not None:
                    acc = add(acc, o, c, sums(halo_both(side, b), turned(o, c), u, v), False)
            for x in range(3):
                force_acc[c, x] = acc[x]

    col_copy().wait_recv()
    for c in range(CL):
        for x in range(3):
            j = 3 * c + x
            value = jnp.sum(force_acc[c, x], axis=0, keepdims=True) + col_in[j : j + 1, :]
            force_acc[c, x] = jnp.broadcast_to(value * DECAY, (8, B))
    atom_sums(0, lambda c, x: force_acc[place[c], x], z_out)
    for copy in z_copies(z_out, z_in, zs, zr):
        copy.start()

    summed = z_sum(dens_out, dens_in, ds, dr)
    for c in range(CL):
        density_ref[pl.ds(place[c], 1), :] = summed[c : c + 1, :]
    fill_buf[...] = summed[0:8] + summed[8:16]
    for copy in fill_copies():
        copy.start()
    results = [
        pltpu.make_async_copy(source, target, osem.at[i])
        for i, (source, target) in enumerate(
            ((density_ref, density_hbm), (fill_buf, fill_in.at[me]), (z_out, z_in.at[z]))
        )
    ]
    for copy in results:
        copy.start()

    @pl.when(has_far)
    def _():
        for copy in far_copies(True):
            copy.wait_recv()

    for copy in z_copies(z_out, z_in, zs, zr, True) + fill_copies(True):
        copy.wait_recv()

    def finish(k, carry):
        halo_copy(k, NEAR).wait_send()
        part_copy(k, NEAR).wait_send()

        @pl.when(has_far)
        def _():
            halo_copy(k, FAR).wait_send()
            part_copy(k, FAR).wait_send()

        return carry

    lax.fori_loop(0, ORDER, finish, 0)
    halo_copy(ORDER, NEAR).wait_send()
    col_copy().wait_send()

    @pl.when(has_far)
    def _():
        halo_copy(ORDER, FAR).wait_send()
        atoms_copy().wait_send()
        for copy in far_copies():
            copy.wait_send()

    for stage in range(2):
        for copy in norm_copies(stage):
            copy.wait_send()
    for copy in fill_copies():
        copy.wait_send()
    for copy in z_copies(dens_out, dens_in, ds, dr) + z_copies(z_out, z_in, zs, zr):
        copy.wait_send()
    for copy in results:
        copy.wait()


def combine(
    clus, probe, density_in, z_hbm, f_hbm, fill_hbm, density_out, filling_out, forces_out,
    z_in, f_in, fill_in, forces, filling, sems,
):
    me = lax.axis_index("clus")
    has_far = jnp.logical_and(me > 0, me < clus - 1)
    arrivals = ((z_hbm, z_in), (fill_hbm, fill_in), (density_in, density_out))
    z_copy, fill_copy, density_copy = [
        pltpu.make_async_copy(source, target, sems.at[i]) for i, (source, target) in enumerate(arrivals)
    ]
    f_copy = pltpu.make_async_copy(f_hbm, f_in, sems.at[3])

    @pl.when(has_far)
    def _():
        f_copy.start()

    @pl.when(jnp.logical_not(has_far))
    def _():
        f_in[...] = jnp.zeros(f_in.shape, F32)

    z_copy.start()
    fill_copy.start()
    density_copy.start()

    @pl.when(has_far)
    def _():
        f_copy.wait()

    z_copy.wait()
    summed = z_in[0]
    for q in range(1, probe):
        summed = summed + z_in[q]
    for q in range(probe):
        summed = summed + f_in[q]
    for quad in range(CL // 4):
        forces[:, quad * B : (quad + 1) * B] = summed[quad * 3 : quad * 3 + 3]
    forces_copy = pltpu.make_async_copy(forces, forces_out, sems.at[4])
    forces_copy.start()
    fill_copy.wait()
    filled = fill_in[0]
    for q in range(1, clus):
        filled = filled + fill_in[q]
    filling[0] = jnp.sum(filled) / (clus * CL * B)
    filling_copy = pltpu.make_async_copy(filling, filling_out, sems.at[5])
    filling_copy.start()
    density_copy.wait()
    forces_copy.wait()
    filling_copy.wait()


def cosines():
    angles = np.pi * (np.arange(QUAD_NODES) + 0.5) / QUAD_NODES
    table = np.zeros((8, B), np.float32)
    for k in range(ORDER + 1):
        table[k, :QUAD_NODES] = np.cos(k * angles)
    return table


def solution(mesh):
    clus, probe = mesh.shape["clus"], mesh.shape["probe"]
    small = 1 + clus // 2
    vmem, dma = pltpu.VMEM, pltpu.SemaphoreType.DMA

    def local(probes, onsite, hopping, block_col, atom_of, bond_dir, chemical_potential):
        in_hbm = pl.BlockSpec(memory_space=pltpu.HBM)
        shapes = (
            jax.ShapeDtypeStruct((CL, B), F32),
            jax.ShapeDtypeStruct((1,), F32),
            jax.ShapeDtypeStruct((3, CL * ATOMS), F32),
        )
        found = pl.pallas_call(
            functools.partial(kernel, clus, probe),
            out_shape=(
                jax.ShapeDtypeStruct((CL, B), F32),
                jax.ShapeDtypeStruct((probe, 16, B), F32),
                jax.ShapeDtypeStruct((probe, 16, B), F32),
                jax.ShapeDtypeStruct((clus, 8, B), F32),
            ),
            in_specs=[in_hbm] * 8,
            out_specs=(in_hbm,) * 4,
            scratch_shapes=[
                vmem((CL, B), F32),
                pltpu.SMEM((1,), F32),
                vmem((CL, ROWS, B), BF16),
                vmem((CL, B), F32),
                vmem((CL, SLOTS), jnp.int32),
                vmem((CL, B), jnp.int32),
                vmem((3, CL, SLOTS), BF16),
                vmem((8, B), F32),
                vmem((CL, B), jnp.int32),
                vmem((EMPTY + 1, B, B), BF16),
                vmem((EMPTY + 1, B, B), BF16),
                vmem((16, B), jnp.int32),
                vmem((48, B), F32),
                pltpu.SMEM((16, B), jnp.int32),
                pltpu.SMEM((48, B), F32),
                vmem((ORDER + 1, CL, ROWS, B), BF16),
                vmem((ORDER + 1, 2, CL, ROWS, B), BF16),
                vmem((ORDER, 2, CL, ROWS, B), LINK),
                vmem((ORDER, 2, CL, ROWS, B), LINK),
                vmem((2, CL, ROWS, B), F32),
                vmem((CL, ROWS, B), F32),
                vmem((CL, ROWS, B), F32),
                vmem((8, B), F32),
                vmem((3, ROWS, B), F32),
                vmem((small, ROWS, B), F32),
                vmem((8, B), F32),
                vmem((16, B), F32),
                vmem((probe, 16, B), F32),
                vmem((CL, 3, 8, B), F32),
                vmem((CL, 3, 8, B), F32),
                vmem((CL * (CL + 1) // 2, 2 * ROWS, B), F32),
                vmem((40, B), F32),
                vmem((40, B), F32),
                vmem((2, CL, B, B), BF16),
                vmem((16, B), F32),
                vmem((16, B), F32),
                dma((7,)),
                dma((3,)),
                dma((SLOTS,)),
                dma((2,)),
                dma((2,)),
                dma((ORDER + 1, 2)),
                dma((ORDER + 1, 2)),
                dma((ORDER, 2)),
                dma((ORDER, 2)),
                dma((small,)),
                dma((small,)),
                dma((clus,)),
                dma((clus,)),
                dma((probe,)),
                dma((probe,)),
                dma((1,)),
                dma((1,)),
                dma((probe,)),
                dma((probe,)),
                dma((probe,)),
                dma((probe,)),
                pltpu.SemaphoreType.REGULAR((4,)),
            ],
            compiler_params=pltpu.CompilerParams(
                collective_id=0, has_side_effects=True, vmem_limit_bytes=60 * 1024 * 1024
            ),
            cost_estimate=pl.CostEstimate(flops=2_600_000_000, bytes_accessed=8_500_000, transcendentals=0),
            name="fermi_forces",
        )(
            probes, onsite, hopping, block_col.T, atom_of, jnp.swapaxes(bond_dir, 1, 2), chemical_potential,
            jnp.asarray(cosines()),
        )
        return pl.pallas_call(
            functools.partial(combine, clus, probe),
            out_shape=shapes,
            in_specs=[in_hbm] * 4,
            out_specs=(in_hbm,) * 3,
            scratch_shapes=[
                vmem((probe, 16, B), F32),
                vmem((probe, 16, B), F32),
                vmem((clus, 8, B), F32),
                vmem((3, CL * ATOMS), F32),
                pltpu.SMEM((1,), F32),
                dma((6,)),
            ],
            compiler_params=pltpu.CompilerParams(vmem_limit_bytes=60 * 1024 * 1024),
            name="combine",
        )(*found)

    return jax.shard_map(
        local,
        mesh=mesh,
        in_specs=(
            P("clus", "probe", None),
            P("clus", None),
            P(None, "clus", None, None),
            P(None, "clus"),
            P("clus", None),
            P(None, None, "clus"),
            P(),
        ),
        out_specs=(P("clus", None), P(), P(None, "clus")),
        check_vma=False,
    )
```
